512 devices in a mesh: wide: 64 (over z, y_hi, core), narrow: 8 (over y_lo, x).
Axes of the slice: x: 4, y: 8 (y_hi: 4, y_lo: 2; y = y_hi * 2 + y_lo), z: 8, core: 2. Of those that a mesh axis runs over, the one named last changes fastest.
Arguments:
- x_tokens: float32 [512, 6144], P('wide', 'narrow'), may hold values from -32 to 32
- grad_out: float32 [512, 6144], P('wide', 'narrow'), may hold values from -32 to 32
- w_in: float32 [6144, 24576], P('narrow', 'wide'), may hold values from -4 to 4
- b_in: float32 [24576], P('wide'), may hold values from -4 to 4
- w_out: float32 [24576, 6144], P('wide', 'narrow'), may hold values from -7 to 7
Outputs:
- grad_in: float32 [512, 6144], P('wide', 'narrow')
- gw_in: float32 [6144, 24576], P('narrow', 'wide')
- gw_out: float32 [24576, 6144], P('wide', 'narrow')
- gb_in: float32 [24576], P('wide')
- gb_out: float32 [6144], P('narrow')
The draws below stay inside these ranges and needn't reach their ends.
All inputs are finite; a program needn't handle non-finite values.
Results may differ from the reference program's by a relative error of at most 0.0003.
Values sent between devices are 32-bit elements; how exact they have to be, the bound alone decides.
A program may use at most 64 MiB of HBM per device.

```python
import math
import jax
import jax.numpy as jnp
from jax import lax

D = 6144
FF = 24576
TOKENS = 512


def rising_scales(key, count, lowest, highest):
    uniform_part = jax.random.uniform(key, (count,), jnp.float32)
    rough = jnp.exp(jnp.log(lowest) + uniform_part * (jnp.log(highest) - jnp.log(lowest)))
    ramp = 3.0 ** (jnp.arange(count, dtype=jnp.float32) / max(count - 1, 1) - 0.5)
    return rough * ramp


def entries(key, shape):
    return jnp.clip(jax.random.normal(key, shape, jnp.float32), -6.0, 6.0)


def draw_x_tokens(key, part):
    key = jax.random.fold_in(key, 11)
    first_key, second_key = jax.random.split(key, 2)
    scales = rising_scales(first_key, D, 0.3, 3.0)
    values = entries(second_key, (TOKENS, D))
    return (values * scales[None, :]).astype(jnp.float32)


def draw_grad_out(key, part):
    key = jax.random.fold_in(key, 23)
    first_key, second_key = jax.random.split(key)
    scales = rising_scales(first_key, D, 0.3, 3.0)
    values = entries(second_key, (TOKENS, D))
    return (values * scales[None, :]).astype(jnp.float32)


def draw_w_in(key, part):
    key = jax.random.fold_in(key, 37)
    first_key, second_key = jax.random.split(key)
    scales = rising_scales(first_key, FF, 0.5, 2.0)
    return (entries(second_key, (D, FF)) * scales[None, :] / jnp.sqrt(jnp.float32(D))).astype(jnp.float32)


def draw_w_out(key, part):
    key = jax.random.fold_in(key, 41)
    first_key, second_key = jax.random.split(key)
    scales = rising_scales(first_key, FF, 0.3, 3.0)
    return (entries(second_key, (FF, D)) * scales[:, None] / jnp.sqrt(jnp.float32(D))).astype(jnp.float32)


def block_levels(key, shape, pieces, least, high):
    loudness = 1.0
    for dim, shards_of in pieces:
        draws = jax.random.uniform(jax.random.fold_in(jax.random.fold_in(key, 6), dim), (shards_of,), jnp.float32, least / len(pieces), high / len(pieces))
        loudness = loudness * jnp.repeat(jnp.exp(draws), shape[dim] // shards_of).reshape((-1,) + (1,) * (len(shape) - 1 - dim))
    return loudness


def scatter_about(own_key, dims, deviation, bound, cuts=(), kind=jnp.bfloat16):
    gain = block_levels(own_key, dims, cuts, -0.22, 0.18) if cuts else 1.0
    array = jax.random.normal(own_key, dims, jnp.float32) * deviation * gain
    return jnp.minimum(jnp.maximum(array, -bound), bound).astype(kind)


def setup_inputs(seed: int = 0) -> dict:
    keys = jax.random.split(jax.random.key(seed), 6)
    return {
        "x_tokens": draw_x_tokens(jax.random.fold_in(keys[5], 71), 0),
        "grad_out": draw_grad_out(jax.random.fold_in(keys[5], 71), 0),
        "w_in": draw_w_in(jax.random.fold_in(keys[5], 71), 0),
        "b_in": scatter_about(keys[3], (FF,), 1.0, 4.0, ((0, 64),), jnp.float32),
        "w_out": draw_w_out(jax.random.fold_in(keys[5], 71), 0),
    }


tanh_scale = math.sqrt(2.0 / math.pi)
cubic_weight = 0.044715

def gelu_parts(pre):
    inner = tanh_scale * (pre + cubic_weight * pre * pre * pre)
    tangent = jnp.tanh(inner)
    value = 0.5 * pre * (1.0 + tangent)
    slope = 0.5 * (1.0 + tangent) + 0.5 * pre * (1.0 - tangent * tangent) * tanh_scale * (1.0 + 3.0 * cubic_weight * pre * pre)
    return (value, slope)

def contract_first(left, right):
    return lax.dot_general(left, right, (((0,), (0,)), ((), ())), precision=lax.Precision.HIGHEST, preferred_element_type=jnp.float32)

def contract_last(left, right):
    return lax.dot_general(left, right, (((1,), (1,)), ((), ())), precision=lax.Precision.HIGHEST, preferred_element_type=jnp.float32)

def reference(x_tokens, grad_out, w_in, b_in, w_out):
    pre = jnp.dot(x_tokens, w_in, precision=lax.Precision.HIGHEST, preferred_element_type=jnp.float32) + b_in
    act, slope = gelu_parts(pre)
    grad_act = contract_last(grad_out, w_out)
    grad_pre = grad_act * slope
    raw_in = contract_first(x_tokens, grad_pre)
    raw_out = contract_first(act, grad_out)
    bias_in = lax.optimization_barrier(jnp.sum(grad_pre, axis=0))
    bias_out = lax.optimization_barrier(jnp.sum(grad_out, axis=0))
    grad_in = contract_last(grad_pre, w_in)
    total = jnp.sum(raw_in * raw_in) + jnp.sum(raw_out * raw_out)
    factor = jnp.minimum(1.0, jnp.sqrt(1.0 * D * FF * TOKENS) / (jnp.sqrt(total) + 1e-06))
    return (grad_in, raw_in * factor, raw_out * factor, bias_in * factor, bias_out * factor)
```

```python
import math

import jax
import jax.numpy as jnp
from jax import lax
from jax.experimental import pallas as pl
from jax.experimental.pallas import tpu as pltpu
from jax.sharding import PartitionSpec as P

D = 6144
FF = 24576
TOKENS = 512
MESH = pl.DeviceIdType.MESH
F32, BF16 = jnp.float32, jnp.bfloat16

NZ, NY, NC, NN = 8, 4, 2, 8
ROWS = 8
BLOCK = NY * NC * ROWS
SENDS = (2, 6, 1, 3, 5, 7, 4)
GROUPS = ((0, 1), (1, 2), (3, 2), (5, 2), (7, 1))
PLACES = ((1, 128), (0, 0), (0, 128), (1, 0), (1, 192))
HALF = 256
FEAT, HID = 768, 384

tanh_scale = math.sqrt(2.0 / math.pi)
cubic_weight = 0.044715


def gelu_parts(pre):
    inner = tanh_scale * (pre + cubic_weight * pre * pre * pre)
    tangent = jnp.tanh(inner)
    value = 0.5 * pre * (1.0 + tangent)
    slope = 0.5 * (1.0 + tangent) + 0.5 * pre * (1.0 - tangent * tangent) * tanh_scale * (
        1.0 + 3.0 * cubic_weight * pre * pre
    )
    return (value, slope)


def split(values):
    high = values.astype(BF16)
    return high, (values - high.astype(F32)).astype(BF16)


def product(left, right):
    return jnp.dot(left, right, preferred_element_type=F32)


def dot3(pair, high, low):
    rows = pair[0].shape[0]
    both = product(jnp.concatenate(pair, axis=0), high)
    return (both[:rows] + both[rows:]) + product(pair[0], low)


def remote(source, target, send, recv, wide, narrow):
    return pltpu.make_async_remote_copy(
        src_ref=source,
        dst_ref=target,
        send_sem=send,
        recv_sem=recv,
        device_id=(wide, narrow),
        device_id_type=MESH,
    )


def drain(ref, sem):
    pltpu.make_async_copy(ref, ref, sem).wait()


def kernel(
    x_ref, g_ref, w_in_ref, b_ref, w_out_ref,
    grad_in_ref, raw_in_ref, raw_out_ref, bias_in_ref, bias_out_ref, factor_ref,
    xg, part, from_narrow, ag, gi, gi_core, gi_z, gi_y, sums,
    w_in_f, w_out_f, w_in_h, w_in_l, w_out_h, w_out_l, w_back_h, w_back_l,
    x_across, g_along, p_along, a_across, bias, b_here,
    load_sem, y_send, y_recv, z_send, z_recv, c_send, c_recv,
    n_send, n_recv, a_send, a_recv, gc_send, gc_recv, gz_send, gz_recv, gy_send, gy_recv,
    s_send, s_recv,
):
    wide = lax.axis_index("wide")
    n = lax.axis_index("narrow")
    z = lax.div(wide, NY * NC)
    y = lax.rem(lax.div(wide, NC), NY)
    c = lax.rem(wide, NC)

    def at(zz, yy, cc):
        return (zz * NY + yy) * NC + cc

    load_in = pltpu.make_async_copy(w_in_ref, w_in_f, load_sem.at[0])
    load_out = pltpu.make_async_copy(w_out_ref, w_out_f, load_sem.at[1])
    load_x = pltpu.make_async_copy(x_ref, xg.at[0, z, c, y], load_sem.at[2])
    load_g = pltpu.make_async_copy(g_ref, xg.at[1, z, c, y], load_sem.at[3])
    load_b = pltpu.make_async_copy(b_ref, b_here, load_sem.at[4])
    for load in (load_x, load_g, load_in, load_out, load_b):
        load.start()

    plane = lax.rem(wide, NY * NC)
    barrier = pltpu.get_barrier_semaphore()
    for j in range(1, 8):
        for peer in (
            (wide, lax.rem(n + j, NN)),
            (z * NY * NC + lax.rem(plane + j, NY * NC), n),
            (lax.rem(z + j, NZ) * NY * NC + plane, n),
        ):
            pl.semaphore_signal(barrier, inc=1, device_id=peer, device_id_type=MESH)
    load_x.wait()
    load_g.wait()
    pl.semaphore_wait(barrier, 21)

    for j in (2, 1, 3):
        own = xg.at[:, z, c, y]
        remote(own, own, y_send, y_recv, at(z, lax.rem(y + j, NY), c), n).start()

    load_in.wait()
    w_in_h[...], w_in_l[...] = split(w_in_f[...])
    load_out.wait()
    w_out_h[...], w_out_l[...] = split(w_out_f[...].T)
    load_b.wait()

    drain(xg.at[:, z, c, pl.ds(0, 3)], y_recv)
    own = xg.at[:, z, c]
    remote(own, own, c_send, c_recv.at[0], at(z, y, 1 - c), n).start()
    remote(own, own, z_send, z_recv.at[1], at(lax.rem(z + 1, NZ), y, c), n).start()
    remote(own, own, z_send, z_recv.at[2], at(lax.rem(z + NZ - 1, NZ), y, c), n).start()

    def block_of(k):
        return lax.rem(z + NZ + (1 - 2 * (k % 2)) * ((k + 1) // 2), NZ)

    def arrive(group):
        first, count = GROUPS[group]
        for k in range(max(first, 1), first + count):
            zb = block_of(k)
            here = xg.at[:, zb, c]
            if k < 7:
                drain(here, z_recv.at[k])
                onward = at(lax.rem(z + NZ - 1 + 2 * (k % 2), NZ), y, c)
                passed = here if k < 5 else xg.at[k - 5, zb, c]
                remote(passed, passed, z_send, z_recv.at[k + 2], onward, n).start()
            else:
                drain(xg.at[0, zb, c], z_recv.at[7])
                drain(xg.at[1, zb, c], z_recv.at[8])
            remote(here, here, c_send, c_recv.at[k], at(z, y, 1 - c), n).start()

    def forward(group):
        first, count = GROUPS[group]
        turn, start = PLACES[group]
        size = count * BLOCK
        blocks = [block_of(k) for k in range(first, first + count)]
        for zb, k in zip(blocks, range(first, first + count)):
            drain(xg.at[:, zb, 1 - c], c_recv.at[k])
        g = jnp.concatenate([xg[1, zb].reshape(BLOCK, FEAT) for zb in blocks], axis=0)
        g_pair = split(g)
        grad_act = dot3(g_pair, w_out_h[...], w_out_l[...])
        x = jnp.concatenate([xg[0, zb].reshape(BLOCK, FEAT) for zb in blocks], axis=0)
        x_pair = split(x)
        pre = dot3(x_pair, w_in_h[...], w_in_l[...])
        for b in range(count):
            rows = slice(b * BLOCK, (b + 1) * BLOCK)
            part[:, first + b, 0] = pre[rows].reshape(NN, ROWS, HID)
            part[:, first + b, 1] = grad_act[rows].reshape(NN, ROWS, HID)
        some = pl.ds(first, count)
        for j in SENDS:
            peer = lax.rem(n + j, NN)
            remote(
                part.at[peer, some], from_narrow.at[j - 1, some], n_send, n_recv.at[group], wide, peer
            ).start()
        across = split(x.T)
        for third, which in enumerate((0, 1, 0)):
            x_across[turn, :, HALF * third + start:HALF * third + start + size] = across[which]
        for third, which in enumerate((0, 0, 1)):
            g_along[turn, HALF * third + start:HALF * third + start + size, :] = g_pair[which]

    def activate(group):
        first, count = GROUPS[group]
        some = pl.ds(first, count)
        drain(from_narrow.at[:, some], n_recv.at[group])
        total = part[n, some]
        for j in range(7):
            total = total + from_narrow[j, some]
        act, slope = gelu_parts(total[:, 0] + b_here[...])
        ag[n, some, 0] = act
        ag[n, some, 1] = total[:, 1] * slope
        mine = ag.at[n, some]
        for j in SENDS:
            remote(mine, mine, a_send, a_recv.at[group], wide, lax.rem(n + j, NN)).start()

    def backward(group):
        first, count = GROUPS[group]
        turn, start = PLACES[group]
        size = count * BLOCK
        drain(ag.at[pl.ds(0, 7), pl.ds(first, count)], a_recv.at[group])
        grad_pre = jnp.concatenate(
            [ag[:, k, 1].reshape(BLOCK, HID) for k in range(first, first + count)], axis=0
        )
        pair = split(grad_pre)
        grad = dot3(pair, w_back_h[...], w_back_l[...])
        gi[pl.ds(first, count)] = grad.reshape(count, NC, NY, ROWS, FEAT)
        some = pl.ds(first, count)
        remote(
            gi.at[some, 1 - c], gi_core.at[some], gc_send, gc_recv.at[group], at(z, y, 1 - c), n
        ).start()
        bias[...] += jnp.sum(grad_pre.reshape(size // 8, 8, HID), axis=0)
        act = jnp.concatenate(
            [ag[:, k, 0].reshape(BLOCK, HID) for k in range(first, first + count)], axis=0
        )
        across = split(act.T)
        for third, which in enumerate((0, 1, 0)):
            a_across[turn, :, HALF * third + start:HALF * third + start + size] = across[which]
        for third, which in enumerate((0, 0, 1)):
            p_along[turn, HALF * third + start:HALF * third + start + size, :] = pair[which]

    def hand_over(group):
        first, count = GROUPS[group]
        drain(gi_core.at[pl.ds(first, count)], gc_recv.at[group])
        for k in range(first, first + count):
            gi[k, c] += gi_core[k]
            if k > 0:
                remote(
                    gi.at[k, c], gi_z.at[k - 1], gz_send, gz_recv, at(block_of(k), y, c), n
                ).start()

    def to_vreg(squares):
        rows, columns = squares.shape
        lanes = jnp.sum(squares.reshape(rows // 8, 8, columns), axis=0)
        out = lanes[:, :128]
        for j in range(1, columns // 128):
            out = out + lanes[:, 128 * j:128 * (j + 1)]
        return out

    def weight_round(turn, size, across, along, raw):
        total = jnp.zeros((8, 128), F32)
        for start in range(0, raw.shape[0], size):
            rows = slice(start, start + size)
            tile = product(across[turn, rows, :], along[turn])
            if turn == 1:
                tile = tile + raw[rows, :]
                total = total + to_vreg(tile * tile)
            raw[rows, :] = tile
        return total

    bias[...] = jnp.zeros_like(bias)
    forward(0)
    arrive(1)
    w_back_h[...], w_back_l[...] = split(w_in_f[...].T)
    forward(1)
    activate(0)
    arrive(2)
    forward(2)
    backward(0)
    activate(1)
    arrive(3)
    forward(3)
    hand_over(0)
    backward(1)
    arrive(4)
    activate(2)
    forward(4)
    hand_over(1)
    backward(2)
    activate(3)
    hand_over(2)
    weight_round(0, 256, x_across, p_along, raw_in_ref)
    weight_round(0, 128, a_across, g_along, raw_out_ref)
    activate(4)
    backward(3)
    hand_over(3)
    backward(4)
    total = weight_round(1, 256, x_across, p_along, raw_in_ref)
    hand_over(4)
    total = total + weight_round(1, 128, a_across, g_along, raw_out_ref)

    def share(phase, place, value, peers):
        sums[phase, place] = value
        for peer in peers:
            slot = sums.at[phase, place]
            remote(slot, slot, s_send, s_recv.at[phase], *peer).start()

    def collect(phase):
        drain(sums.at[phase, pl.ds(0, 7)], s_recv.at[phase])
        return jnp.sum(sums[phase], axis=0)

    share(0, n, total, [(wide, lax.rem(n + j, NN)) for j in range(1, 8)])

    drain(gi_z, gz_recv)
    own_sum = gi[0, c]
    for j in range(7):
        own_sum = own_sum + gi_z[j]
    gi[0, c] = own_sum
    for j in (2, 1, 3):
        to = lax.rem(y + j, NY)
        remote(gi.at[0, c, to], gi_y.at[j - 1], gy_send, gy_recv, at(z, to, c), n).start()

    total = collect(0)
    share(1, plane, total, [
        (z * NY * NC + lax.rem(plane + j, NY * NC), n) for j in range(1, 8)
    ])
    bias_in_ref[...] = jnp.sum(bias[...], axis=0, keepdims=True)
    bias_out_ref[...] = jnp.sum(xg[1].reshape(TOKENS, FEAT), axis=0, keepdims=True)
    total = collect(1)
    share(2, z, total, [
        (lax.rem(z + j, NZ) * NY * NC + plane, n) for j in range(1, 8)
    ])
    drain(gi_y, gy_recv)
    grad_in_ref[...] = (gi[0, c, y] + gi_y[0]) + (gi_y[1] + gi_y[2])
    drain(xg.at[:, z, c, pl.ds(0, 3)], y_send)
    drain(xg.at[:, pl.ds(0, 7), 0], z_send)
    drain(xg.at[:, :, 0], c_send)
    drain(from_narrow, n_send)
    drain(ag.at[pl.ds(0, 7)], a_send)
    drain(gi_core, gc_send)
    drain(gi_z, gz_send)
    drain(gi_y, gy_send)
    total = jnp.sum(collect(2), keepdims=True)
    factor = jnp.minimum(1.0, math.sqrt(1.0 * D * FF * TOKENS) / (jnp.sqrt(total) + 1e-06))
    factor_ref[...] = jnp.broadcast_to(factor, factor_ref.shape)
    drain(sums.at[:, pl.ds(0, 7)], s_send)


PIECES = 3


def scale_kernel(
    grad_in_ref, raw_in_ref, raw_out_ref, bias_in_ref, bias_out_ref, factor_ref,
    grad_in_out, gw_in, gw_out, gb_in, gb_out, buf_in, buf_out, sems,
):
    factor = factor_ref[0:1, 0:1]
    stores = []
    for which, (raw, buf, out) in enumerate(
        ((raw_in_ref, buf_in, gw_in), (raw_out_ref, buf_out, gw_out))
    ):
        size = raw.shape[0] // PIECES
        for i in range(PIECES):
            rows = pl.ds(i * size, size)
            buf[rows, :] = raw[rows, :] * factor
            store = pltpu.make_async_copy(buf.at[rows], out.at[rows], sems.at[which, i])
            store.start()
            stores.append(store)
    grad_in_out[...] = grad_in_ref[...]
    gb_in[...] = (bias_in_ref[...] * factor)[0]
    gb_out[...] = (bias_out_ref[...] * factor)[0]
    for store in stores:
        store.wait()


def local(x_tokens, grad_out, w_in, b_in, w_out):
    vmem = pl.BlockSpec(memory_space=pltpu.VMEM)
    anywhere = pl.BlockSpec(memory_space=pl.ANY)
    dma = pltpu.SemaphoreType.DMA
    grad_in, raw_in, raw_out, bias_in, bias_out, factor = pl.pallas_call(
        kernel,
        out_shape=(
            jax.ShapeDtypeStruct((ROWS, FEAT), F32),
            jax.ShapeDtypeStruct((FEAT, HID), F32),
            jax.ShapeDtypeStruct((HID, FEAT), F32),
            jax.ShapeDtypeStruct((1, HID), F32),
            jax.ShapeDtypeStruct((1, FEAT), F32),
            jax.ShapeDtypeStruct((8, 128), F32),
        ),
        in_specs=[pl.BlockSpec(memory_space=pltpu.HBM)] * 5,
        out_specs=(vmem, vmem, vmem, vmem, vmem, vmem),
        scratch_shapes=[
            pltpu.VMEM((2, NZ, NC, NY, ROWS, FEAT), F32),
            pltpu.VMEM((NN, NZ, 2, ROWS, HID), F32),
            pltpu.VMEM((NN - 1, NZ, 2, ROWS, HID), F32),
            pltpu.VMEM((NN, NZ, 2, ROWS, HID), F32),
            pltpu.VMEM((NZ, NC, NY, ROWS, FEAT), F32),
            pltpu.VMEM((NZ, NY, ROWS, FEAT), F32),
            pltpu.VMEM((NZ - 1, NY, ROWS, FEAT), F32),
            pltpu.VMEM((NY - 1, ROWS, FEAT), F32),
            pltpu.VMEM((3, 8, 8, 128), F32),
            pltpu.VMEM((FEAT, HID), F32),
            pltpu.VMEM((HID, FEAT), F32),
            pltpu.VMEM((FEAT, HID), BF16),
            pltpu.VMEM((FEAT, HID), BF16),
            pltpu.VMEM((FEAT, HID), BF16),
            pltpu.VMEM((FEAT, HID), BF16),
            pltpu.VMEM((HID, FEAT), BF16),
            pltpu.VMEM((HID, FEAT), BF16),
            pltpu.VMEM((2, FEAT, 3 * HALF), BF16),
            pltpu.VMEM((2, 3 * HALF, FEAT), BF16),
            pltpu.VMEM((2, 3 * HALF, HID), BF16),
            pltpu.VMEM((2, HID, 3 * HALF), BF16),
            pltpu.VMEM((ROWS, HID), F32),
            pltpu.VMEM((HID,), F32),
            dma((5,)),
            dma, dma,
            dma, dma((9,)),
            dma, dma((NZ,)),
            dma, dma((NZ,)),
            dma, dma((NZ,)),
            dma, dma((NZ,)),
            dma, dma,
            dma, dma,
            dma, dma((3,)),
        ],
        compiler_params=pltpu.CompilerParams(
            collective_id=0, has_side_effects=True, vmem_limit_bytes=51 * 1024 * 1024
        ),
    )(x_tokens, grad_out, w_in, b_in, w_out)
    return pl.pallas_call(
        scale_kernel,
        out_shape=(
            jax.ShapeDtypeStruct((ROWS, FEAT), F32),
            jax.ShapeDtypeStruct((FEAT, HID), F32),
            jax.ShapeDtypeStruct((HID, FEAT), F32),
            jax.ShapeDtypeStruct((HID,), F32),
            jax.ShapeDtypeStruct((FEAT,), F32),
        ),
        in_specs=[vmem, vmem, vmem, vmem, vmem, vmem],
        out_specs=(vmem, anywhere, anywhere, vmem, vmem),
        scratch_shapes=[
            pltpu.VMEM((FEAT, HID), F32),
            pltpu.VMEM((HID, FEAT), F32),
            dma((2, PIECES)),
        ],
        compiler_params=pltpu.CompilerParams(vmem_limit_bytes=16 * 1024 * 1024),
    )(grad_in, raw_in, raw_out, bias_in, bias_out, factor)


def solution(mesh):
    placed = (
        P("wide", "narrow"),
        P("wide", "narrow"),
        P("narrow", "wide"),
        P("wide"),
        P("wide", "narrow"),
    )
    return jax.shard_map(
        local,
        mesh=mesh,
        in_specs=placed,
        out_specs=(
            P("wide", "narrow"),
            P("narrow", "wide"),
            P("wide", "narrow"),
            P("wide"),
            P("narrow"),
        ),
        check_vma=False,
    )
```

```python
import math

import jax
import jax.numpy as jnp
from jax import lax
from jax.experimental import pallas as pl
from jax.experimental.pallas import tpu as pltpu
from jax.sharding import PartitionSpec as P

D = 6144
FF = 24576
TOKENS = 512
MESH = pl.DeviceIdType.MESH
F32, BF16 = jnp.float32, jnp.bfloat16

NZ, NY, NC, NN = 8, 4, 2, 8
ROWS = 8
BLOCK = NY * NC * ROWS
NX = 4
GROUPS = ((0, 1), (1, 2), (3, 2), (5, 2), (7, 1))
PLACES = ((1, 128), (0, 0), (0, 128), (1, 0), (1, 192))
HALF = 256
FIRST_Y = 5
STEPS = (
    "10a1200130a2", "11024021a312", "3103a4504122", "041332605114", "702342613352", "247143346253",
)
FEAT, HID = 768, 384

tanh_scale = math.sqrt(2.0 / math.pi)
cubic_weight = 0.044715


def gelu_parts(pre):
    inner = tanh_scale * (pre + cubic_weight * pre * pre * pre)
    tangent = jnp.tanh(inner)
    value = 0.5 * pre * (1.0 + tangent)
    slope = 0.5 * (1.0 + tangent) + 0.5 * pre * (1.0 - tangent * tangent) * tanh_scale * (
        1.0 + 3.0 * cubic_weight * pre * pre
    )
    return (value, slope)


def split(values):
    high = values.astype(BF16)
    return high, (values - high.astype(F32)).astype(BF16)


def product(left, right):
    return jnp.dot(left, right, preferred_element_type=F32)


def dot3(pair, high, low):
    rows = pair[0].shape[0]
    both = product(jnp.concatenate(pair, axis=0), high)
    return (both[:rows] + both[rows:]) + product(pair[0], low)


def remote(source, target, send, recv, wide, narrow):
    return pltpu.make_async_remote_copy(
        src_ref=source,
        dst_ref=target,
        send_sem=send,
        recv_sem=recv,
        device_id=(wide, narrow),
        device_id_type=MESH,
    )


def drain(ref, sem):
    pltpu.make_async_copy(ref, ref, sem).wait()


def kernel(
    x_ref, g_ref, w_in_ref, b_ref, w_out_ref,
    grad_in_ref, raw_in_ref, raw_out_ref, bias_in_ref, bias_out_ref, factor_ref,
    xg, part, relay, near, across_y, ag, gi, gi_core, gi_z, gi_y, gi_y_first, gi_z_last, sums,
    w_in_f, w_out_f, w_in_h, w_in_l, w_out_h, w_out_l, w_back_h, w_back_l,
    x_across, g_along, p_along, a_across, bias, b_here,
    load_sem, y_send, y_recv, z_send, z_recv, c_send, c_recv,
    f_send, f_recv, n_send, n_recv, s_y_send, s_y_recv, a_send, a_y_recv, a_one_recv, a_two_recv, a_far_recv,
    gc_send, gc_recv, gz_send, gz_recv, gy_send, gy_recv, gyf_send, gyf_recv, gzl_send, gzl_recv,
    s_send, s_recv,
):
    wide = lax.axis_index("wide")
    n = lax.axis_index("narrow")
    z = lax.div(wide, NY * NC)
    y = lax.rem(lax.div(wide, NC), NY)
    c = lax.rem(wide, NC)

    yl = lax.div(n, NX)
    x = lax.rem(n, NX)
    right, left, far = (lax.rem(x + j, NX) for j in (1, 3, 2))
    over = (1 - yl) * NX + x

    def at(zz, yy, cc):
        return (zz * NY + yy) * NC + cc

    load_in = pltpu.make_async_copy(w_in_ref, w_in_f, load_sem.at[0])
    load_out = pltpu.make_async_copy(w_out_ref, w_out_f, load_sem.at[1])
    load_x = pltpu.make_async_copy(x_ref, xg.at[0, z, c, y], load_sem.at[2])
    load_g = pltpu.make_async_copy(g_ref, xg.at[1, z, c, y], load_sem.at[3])
    load_b = pltpu.make_async_copy(b_ref, b_here, load_sem.at[4])
    for load in (load_x, load_g, load_in, load_out, load_b):
        load.start()

    plane = lax.rem(wide, NY * NC)
    barrier = pltpu.get_barrier_semaphore()
    for j in range(1, 8):
        for peer in (
            (wide, lax.rem(n + j, NN)),
            (z * NY * NC + lax.rem(plane + j, NY * NC), n),
            (lax.rem(z + j, NZ) * NY * NC + plane, n),
        ):
            pl.semaphore_signal(barrier, inc=1, device_id=peer, device_id_type=MESH)
    load_x.wait()
    load_g.wait()
    pl.semaphore_wait(barrier, 21)

    for j in (2, 1, 3):
        own = xg.at[:, z, c, y]
        remote(own, own, y_send, y_recv, at(z, lax.rem(y + j, NY), c), n).start()

    load_in.wait()
    w_in_h[...], w_in_l[...] = split(w_in_f[...])
    load_out.wait()
    w_out_h[...], w_out_l[...] = split(w_out_f[...].T)
    load_b.wait()

    drain(xg.at[:, z, c, pl.ds(0, 3)], y_recv)
    own = xg.at[:, z, c]
    remote(own, own, c_send, c_recv.at[0], at(z, y, 1 - c), n).start()
    remote(own, own, z_send, z_recv.at[1], at(lax.rem(z + 1, NZ), y, c), n).start()
    remote(own, own, z_send, z_recv.at[2], at(lax.rem(z + NZ - 1, NZ), y, c), n).start()

    def block_of(k):
        return lax.rem(z + NZ + (1 - 2 * (k % 2)) * ((k + 1) // 2), NZ)

    def arrive(group):
        first, count = GROUPS[group]
        for k in range(max(first, 1), first + count):
            zb = block_of(k)
            here = xg.at[:, zb, c]
            if k < 7:
                drain(here, z_recv.at[k])
                onward = at(lax.rem(z + NZ - 1 + 2 * (k % 2), NZ), y, c)
                passed = here if k < 5 else xg.at[k - 5, zb, c]
                remote(passed, passed, z_send, z_recv.at[k + 2], onward, n).start()
            else:
                drain(xg.at[0, zb, c], z_recv.at[7])
                drain(xg.at[1, zb, c], z_recv.at[8])
            remote(here, here, c_send, c_recv.at[k], at(z, y, 1 - c), n).start()

    def forward(group):
        first, count = GROUPS[group]
        turn, start = PLACES[group]
        size = count * BLOCK
        blocks = [block_of(k) for k in range(first, first + count)]
        for zb, k in zip(blocks, range(first, first + count)):
            drain(xg.at[:, zb, 1 - c], c_recv.at[k])
        g_rows = jnp.concatenate([xg[1, zb].reshape(BLOCK, FEAT) for zb in blocks], axis=0)
        g_pair = split(g_rows)
        grad_act = dot3(g_pair, w_out_h[...], w_out_l[...])
        x_rows = jnp.concatenate([xg[0, zb].reshape(BLOCK, FEAT) for zb in blocks], axis=0)
        x_pair = split(x_rows)
        pre = dot3(x_pair, w_in_h[...], w_in_l[...])
        for b in range(count):
            rows = slice(b * BLOCK, (b + 1) * BLOCK)
            part[:, first + b, 0] = pre[rows].reshape(NN, ROWS, HID)
            part[:, first + b, 1] = grad_act[rows].reshape(NN, ROWS, HID)
        some = pl.ds(first, count)
        to_right, to_left = yl * NX + right, yl * NX + left
        remote(part.at[far, some], relay.at[0, some], f_send, f_recv.at[group], wide, to_right).start()
        remote(part.at[NX + far, some], relay.at[1, some], f_send, f_recv.at[group], wide, to_left).start()
        remote(part.at[NX + right, some], near.at[0, 1, some], n_send, n_recv.at[group], wide, to_right).start()
        remote(part.at[left, some], near.at[1, 0, some], n_send, n_recv.at[group], wide, to_left).start()
        across = split(x_rows.T)
        for third, which in enumerate((0, 1, 0)):
            x_across[turn, :, HALF * third + start:HALF * third + start + size] = across[which]
        for third, which in enumerate((0, 0, 1)):
            g_along[turn, HALF * third + start:HALF * third + start + size, :] = g_pair[which]

    def pass_on(group):
        some = pl.ds(*GROUPS[group])
        drain(relay.at[:, some], f_recv.at[group])
        part[right, some] += relay[0, some]
        part[NX + left, some] += relay[1, some]
        remote(
            part.at[right, some], near.at[0, 0, some], n_send, n_recv.at[group], wide, yl * NX + right
        ).start()
        remote(
            part.at[NX + left, some], near.at[1, 1, some], n_send, n_recv.at[group], wide, yl * NX + left
        ).start()

    def add_x(group):
        some = pl.ds(*GROUPS[group])
        drain(near.at[:, :, some], n_recv.at[group])
        part[over, some] += near[0, 1 - yl, some] + near[1, 1 - yl, some]
        remote(
            part.at[over, some], across_y.at[some], s_y_send, s_y_recv.at[group], wide, over
        ).start()
        part[n, some] += near[0, yl, some] + near[1, yl, some]

    def activate(group):
        some = pl.ds(*GROUPS[group])
        drain(across_y.at[some], s_y_recv.at[group])
        total = part[n, some] + across_y[some]
        act, slope = gelu_parts(total[:, 0] + b_here[...])
        ag[n, some, 0] = act
        ag[n, some, 1] = total[:, 1] * slope
        mine = ag.at[n, some]
        remote(mine, mine, a_send, a_y_recv.at[group], wide, over).start()
        for side in (right, left):
            remote(mine, mine, a_send, a_one_recv.at[group], wide, yl * NX + side).start()

    ahead = lax.rem(x + 1 + 2 * yl, NX)
    behind = lax.rem(x + 3 - 2 * yl, NX)

    def spread(group):
        some = pl.ds(*GROUPS[group])
        drain(across_y.at[some], a_y_recv.at[group])
        other = ag.at[over, some]
        for side in (right, left):
            remote(other, other, a_send, a_two_recv.at[group], wide, yl * NX + side).start()
        drain(ag.at[pl.ds(0, 2), some], a_one_recv.at[group])
        chunk = ag.at[yl * NX + behind, some]
        remote(chunk, chunk, a_send, a_far_recv.at[group], wide, yl * NX + ahead).start()

    def spread_far(group):
        some = pl.ds(*GROUPS[group])
        drain(ag.at[pl.ds(0, 2), some], a_two_recv.at[group])
        chunk = ag.at[(1 - yl) * NX + ahead, some]
        remote(chunk, chunk, a_send, a_far_recv.at[group], wide, yl * NX + behind).start()

    def backward(group):
        first, count = GROUPS[group]
        turn, start = PLACES[group]
        size = count * BLOCK
        drain(ag.at[pl.ds(0, 2), pl.ds(first, count)], a_far_recv.at[group])
        grad_pre = jnp.concatenate(
            [ag[:, k, 1].reshape(BLOCK, HID) for k in range(first, first + count)], axis=0
        )
        pair = split(grad_pre)
        grad = dot3(pair, w_back_h[...], w_back_l[...])
        gi[pl.ds(first, count)] = grad.reshape(count, NC, NY, ROWS, FEAT)
        some = pl.ds(first, count)
        remote(
            gi.at[some, 1 - c], gi_core.at[some], gc_send, gc_recv.at[group], at(z, y, 1 - c), n
        ).start()
        bias[...] += jnp.sum(grad_pre.reshape(size // 8, 8, HID), axis=0)
        act = jnp.concatenate(
            [ag[:, k, 0].reshape(BLOCK, HID) for k in range(first, first + count)], axis=0
        )
        across = split(act.T)
        for third, which in enumerate((0, 1, 0)):
            a_across[turn, :, HALF * third + start:HALF * third + start + size] = across[which]
        for third, which in enumerate((0, 0, 1)):
            p_along[turn, HALF * third + start:HALF * third + start + size, :] = pair[which]

    def hand_over(group):
        first, count = GROUPS[group]
        drain(gi_core.at[pl.ds(first, count)], gc_recv.at[group])
        for k in range(first, first + count):
            gi[k, c] += gi_core[k]
            if 0 < k < FIRST_Y:
                remote(
                    gi.at[k, c], gi_z.at[k - 1], gz_send, gz_recv, at(block_of(k), y, c), n
                ).start()
        if first >= FIRST_Y:
            for j in (2, 1, 3):
                to = lax.rem(y + j, NY)
                remote(
                    gi.at[pl.ds(first, count), c, to],
                    gi_y_first.at[j - 1, pl.ds(first - FIRST_Y, count)],
                    gyf_send, gyf_recv.at[group - 3], at(z, to, c), n,
                ).start()

    def to_owner(group):
        first, count = GROUPS[group]
        drain(gi_y_first.at[:, pl.ds(first - FIRST_Y, count)], gyf_recv.at[group - 3])
        for k in range(first, first + count):
            i = k - FIRST_Y
            gi[k, c, y] += gi_y_first[0, i] + (gi_y_first[1, i] + gi_y_first[2, i])
            remote(
                gi.at[k, c, y], gi_z_last.at[i], gzl_send, gzl_recv, at(block_of(k), y, c), n
            ).start()

    def to_vreg(squares):
        rows, columns = squares.shape
        lanes = jnp.sum(squares.reshape(rows // 8, 8, columns), axis=0)
        out = lanes[:, :128]
        for j in range(1, columns // 128):
            out = out + lanes[:, 128 * j:128 * (j + 1)]
        return out

    def weight_round(turn, size, across, along, raw):
        total = jnp.zeros((8, 128), F32)
        for start in range(0, raw.shape[0], size):
            rows = slice(start, start + size)
            tile = product(across[turn, rows, :], along[turn])
            if turn == 1:
                tile = tile + raw[rows, :]
                total = total + to_vreg(tile * tile)
            raw[rows, :] = tile
        return total

    bias[...] = jnp.zeros_like(bias)
    stages = {
        "a": arrive, "0": forward, "1": pass_on, "2": add_x, "3": activate, "4": spread,
        "5": spread_far, "6": backward, "7": hand_over, "8": to_owner,
    }

    def run(order):
        for stage, group in zip(order[::2], order[1::2]):
            stages[stage](int(group))

    run("00")
    w_back_h[...], w_back_l[...] = split(w_in_f[...].T)
    for order in STEPS:
        run(order)
    weight_round(0, 256, x_across, p_along, raw_in_ref)
    run("4463725473")
    weight_round(0, 128, a_across, g_along, raw_out_ref)
    run("6483")
    total = weight_round(1, 256, x_across, p_along, raw_in_ref)
    run("74")
    total = total + weight_round(1, 128, a_across, g_along, raw_out_ref)

    def share(phase, place, value, peers):
        sums[phase, place] = value
        for peer in peers:
            slot = sums.at[phase, place]
            remote(slot, slot, s_send, s_recv.at[phase], *peer).start()

    def collect(phase):
        drain(sums.at[phase, pl.ds(0, 7)], s_recv.at[phase])
        return jnp.sum(sums[phase], axis=0)

    share(0, n, total, [(wide, lax.rem(n + j, NN)) for j in range(1, 8)])

    to_owner(4)
    drain(gi_z, gz_recv)
    own_sum = gi[0, c]
    for j in range(FIRST_Y - 1):
        own_sum = own_sum + gi_z[j]
    gi[0, c] = own_sum
    for j in (2, 1, 3):
        to = lax.rem(y + j, NY)
        remote(gi.at[0, c, to], gi_y.at[j - 1], gy_send, gy_recv, at(z, to, c), n).start()

    total = collect(0)
    share(1, plane, total, [
        (z * NY * NC + lax.rem(plane + j, NY * NC), n) for j in range(1, 8)
    ])
    bias_in_ref[...] = jnp.sum(bias[...], axis=0, keepdims=True)
    bias_out_ref[...] = jnp.sum(xg[1].reshape(TOKENS, FEAT), axis=0, keepdims=True)
    total = collect(1)
    share(2, z, total, [
        (lax.rem(z + j, NZ) * NY * NC + plane, n) for j in range(1, 8)
    ])
    drain(gi_y, gy_recv)
    drain(gi_z_last, gzl_recv)
    grad_in_ref[...] = ((gi[0, c, y] + gi_y[0]) + (gi_y[1] + gi_y[2])) + (
        (gi_z_last[0] + gi_z_last[1]) + gi_z_last[2]
    )
    drain(xg.at[:, z, c, pl.ds(0, 3)], y_send)
    drain(xg.at[:, pl.ds(0, 7), 0], z_send)
    drain(xg.at[:, :, 0], c_send)
    drain(relay, f_send)
    drain(near, n_send)
    drain(across_y, s_y_send)
    drain(ag.at[pl.ds(0, 7)], a_send)
    drain(gi_core, gc_send)
    drain(gi_z, gz_send)
    drain(gi_y, gy_send)
    drain(gi_y_first, gyf_send)
    drain(gi_z_last, gzl_send)
    total = jnp.sum(collect(2), keepdims=True)
    factor = jnp.minimum(1.0, math.sqrt(1.0 * D * FF * TOKENS) / (jnp.sqrt(total) + 1e-06))
    factor_ref[...] = jnp.broadcast_to(factor, factor_ref.shape)
    drain(sums.at[:, pl.ds(0, 7)], s_send)


PIECES = 3


def scale_kernel(
    grad_in_ref, raw_in_ref, raw_out_ref, bias_in_ref, bias_out_ref, factor_ref,
    grad_in_out, gw_in, gw_out, gb_in, gb_out, buf_in, buf_out, sems,
):
    factor = factor_ref[0:1, 0:1]
    stores = []
    for which, (raw, buf, out) in enumerate(
        ((raw_in_ref, buf_in, gw_in), (raw_out_ref, buf_out, gw_out))
    ):
        size = raw.shape[0] // PIECES
        for i in range(PIECES):
            rows = pl.ds(i * size, size)
            buf[rows, :] = raw[rows, :] * factor
            store = pltpu.make_async_copy(buf.at[rows], out.at[rows], sems.at[which, i])
            store.start()
            stores.append(store)
    grad_in_out[...] = grad_in_ref[...]
    gb_in[...] = (bias_in_ref[...] * factor)[0]
    gb_out[...] = (bias_out_ref[...] * factor)[0]
    for store in stores:
        store.wait()


def local(x_tokens, grad_out, w_in, b_in, w_out):
    vmem = pl.BlockSpec(memory_space=pltpu.VMEM)
    anywhere = pl.BlockSpec(memory_space=pl.ANY)
    dma = pltpu.SemaphoreType.DMA
    grad_in, raw_in, raw_out, bias_in, bias_out, factor = pl.pallas_call(
        kernel,
        out_shape=(
            jax.ShapeDtypeStruct((ROWS, FEAT), F32),
            jax.ShapeDtypeStruct((FEAT, HID), F32),
            jax.ShapeDtypeStruct((HID, FEAT), F32),
            jax.ShapeDtypeStruct((1, HID), F32),
            jax.ShapeDtypeStruct((1, FEAT), F32),
            jax.ShapeDtypeStruct((8, 128), F32),
        ),
        in_specs=[pl.BlockSpec(memory_space=pltpu.HBM)] * 5,
        out_specs=(vmem, vmem, vmem, vmem, vmem, vmem),
        scratch_shapes=[
            pltpu.VMEM((2, NZ, NC, NY, ROWS, FEAT), F32),
            pltpu.VMEM((NN, NZ, 2, ROWS, HID), F32),
            pltpu.VMEM((2, NZ, 2, ROWS, HID), F32),
            pltpu.VMEM((2, 2, NZ, 2, ROWS, HID), F32),
            pltpu.VMEM((NZ, 2, ROWS, HID), F32),
            pltpu.VMEM((NN, NZ, 2, ROWS, HID), F32),
            pltpu.VMEM((NZ, NC, NY, ROWS, FEAT), F32),
            pltpu.VMEM((NZ, NY, ROWS, FEAT), F32),
            pltpu.VMEM((FIRST_Y - 1, NY, ROWS, FEAT), F32),
            pltpu.VMEM((NY - 1, ROWS, FEAT), F32),
            pltpu.VMEM((NY - 1, NZ - FIRST_Y, ROWS, FEAT), F32),
            pltpu.VMEM((NZ - FIRST_Y, ROWS, FEAT), F32),
            pltpu.VMEM((3, 8, 8, 128), F32),
            pltpu.VMEM((FEAT, HID), F32),
            pltpu.VMEM((HID, FEAT), F32),
            pltpu.VMEM((FEAT, HID), BF16),
            pltpu.VMEM((FEAT, HID), BF16),
            pltpu.VMEM((FEAT, HID), BF16),
            pltpu.VMEM((FEAT, HID), BF16),
            pltpu.VMEM((HID, FEAT), BF16),
            pltpu.VMEM((HID, FEAT), BF16),
            pltpu.VMEM((2, FEAT, 3 * HALF), BF16),
            pltpu.VMEM((2, 3 * HALF, FEAT), BF16),
            pltpu.VMEM((2, 3 * HALF, HID), BF16),
            pltpu.VMEM((2, HID, 3 * HALF), BF16),
            pltpu.VMEM((ROWS, HID), F32),
            pltpu.VMEM((HID,), F32),
            dma((5,)),
            dma, dma,
            dma, dma((9,)),
            dma, dma((NZ,)),
            dma, dma((5,)),
            dma, dma((5,)),
            dma, dma((5,)),
            dma, dma((5,)), dma((5,)), dma((5,)), dma((5,)),
            dma, dma((5,)),
            dma, dma,
            dma, dma,
            dma, dma((2,)),
            dma, dma,
            dma, dma((3,)),
        ],
        compiler_params=pltpu.CompilerParams(
            collective_id=0, has_side_effects=True, vmem_limit_bytes=51 * 1024 * 1024
        ),
    )(x_tokens, grad_out, w_in, b_in, w_out)
    return pl.pallas_call(
        scale_kernel,
        out_shape=(
            jax.ShapeDtypeStruct((ROWS, FEAT), F32),
            jax.ShapeDtypeStruct((FEAT, HID), F32),
            jax.ShapeDtypeStruct((HID, FEAT), F32),
            jax.ShapeDtypeStruct((HID,), F32),
            jax.ShapeDtypeStruct((FEAT,), F32),
        ),
        in_specs=[vmem, vmem, vmem, vmem, vmem, vmem],
        out_specs=(vmem, anywhere, anywhere, vmem, vmem),
        scratch_shapes=[
            pltpu.VMEM((FEAT, HID), F32),
            pltpu.VMEM((HID, FEAT), F32),
            dma((2, PIECES)),
        ],
        compiler_params=pltpu.CompilerParams(vmem_limit_bytes=16 * 1024 * 1024),
    )(grad_in, raw_in, raw_out, bias_in, bias_out, factor)


def solution(mesh):
    placed = (
        P("wide", "narrow"),
        P("wide", "narrow"),
        P("narrow", "wide"),
        P("wide"),
        P("wide", "narrow"),
    )
    return jax.shard_map(
        local,
        mesh=mesh,
        in_specs=placed,
        out_specs=(
            P("wide", "narrow"),
            P("narrow", "wide"),
            P("wide", "narrow"),
            P("wide"),
            P("narrow"),
        ),
        check_vma=False,
    )
```

```python
import math

import jax
import jax.numpy as jnp
from jax import lax
from jax.experimental import pallas as pl
from jax.experimental.pallas import tpu as pltpu
from jax.sharding import PartitionSpec as P

D = 6144
FF = 24576
TOKENS = 512
MESH = pl.DeviceIdType.MESH
F32, BF16 = jnp.float32, jnp.bfloat16

NZ, NY, NC, NN = 8, 4, 2, 8
ROWS = 8
BLOCK = NY * NC * ROWS
NX = 4
GROUPS = ((0, 1), (1, 2), (3, 2), (5, 2), (7, 1))
PLACES = ((1152, 128, 0), (0, 256, 0), (0, 256, 128), (768, 128, 0), (1152, 128, 64))
ROUNDS = ((0, 768), (768, 384), (1152, 384))
SUM_COLUMNS = 1536
FIRST_Y = 7
STEPS = (
    "x0h110a1h22001x1a230h31102x2a340h4211203a450x331220413x460b0",
    "3241147023425133245261b1433462b2v0537172446354b3v17364b4",
)
FEAT, HID = 768, 384

tanh_scale = math.sqrt(2.0 / math.pi)
cubic_weight = 0.044715


def gelu_parts(pre):
    inner = tanh_scale * (pre + cubic_weight * pre * pre * pre)
    tangent = jnp.tanh(inner)
    value = 0.5 * pre * (1.0 + tangent)
    slope = 0.5 * (1.0 + tangent) + 0.5 * pre * (1.0 - tangent * tangent) * tanh_scale * (
        1.0 + 3.0 * cubic_weight * pre * pre
    )
    return (value, slope)


def split(values):
    high = values.astype(BF16)
    return high, (values - high.astype(F32)).astype(BF16)


def product(left, right):
    return jnp.dot(left, right, preferred_element_type=F32)


def dot3(pair, high, low):
    rows = pair[0].shape[0]
    both = product(jnp.concatenate(pair, axis=0), high)
    return (both[:rows] + both[rows:]) + product(pair[0], low)


def remote(source, target, send, recv, wide, narrow):
    return pltpu.make_async_remote_copy(
        src_ref=source,
        dst_ref=target,
        send_sem=send,
        recv_sem=recv,
        device_id=(wide, narrow),
        device_id_type=MESH,
    )


def drain(ref, sem):
    pltpu.make_async_copy(ref, ref, sem).wait()


def kernel(
    x_ref, g_ref, w_in_ref, b_ref, w_out_ref,
    grad_in_ref, raw_in_ref, raw_out_ref, bias_in_ref, bias_out_ref, factor_ref,
    xg, part, relay, near, across_y, ag, gi, gi_core, gi_z, gi_y, gi_y_first, gi_z_last, sums,
    w_in_f, w_out_f, w_in_h, w_in_l, w_out_h, w_out_l, w_back_h, w_back_l,
    x_across, g_along, p_along, a_across, bias, b_here,
    load_sem, y_send, y_recv, z_send, z_recv, c_send, c_recv,
    f_send, f_recv, n_send, n_recv, s_y_send, s_y_recv, a_send, a_y_recv, a_one_recv, a_two_recv, a_far_recv,
    gc_send, gc_recv, gz_send, gz_recv, gy_send, gy_recv, gyf_send, gyf_recv, gzl_send, gzl_recv,
    s_send, s_recv,
):
    wide = lax.axis_index("wide")
    n = lax.axis_index("narrow")
    z = lax.div(wide, NY * NC)
    y = lax.rem(lax.div(wide, NC), NY)
    c = lax.rem(wide, NC)

    yl = lax.div(n, NX)
    x = lax.rem(n, NX)
    right, left, far = (lax.rem(x + j, NX) for j in (1, 3, 2))
    over = (1 - yl) * NX + x

    def at(zz, yy, cc):
        return (zz * NY + yy) * NC + cc

    load_in = pltpu.make_async_copy(w_in_ref, w_in_f, load_sem.at[0])
    load_out = pltpu.make_async_copy(w_out_ref, w_out_f, load_sem.at[1])
    load_x = pltpu.make_async_copy(x_ref, xg.at[0, z, c, y], load_sem.at[2])
    load_g = pltpu.make_async_copy(g_ref, xg.at[1, z, c, y], load_sem.at[3])
    load_b = pltpu.make_async_copy(b_ref, b_here, load_sem.at[4])
    for load in (load_x, load_g, load_in, load_out, load_b):
        load.start()

    plane = lax.rem(wide, NY * NC)
    barrier = pltpu.get_barrier_semaphore()
    for j in range(1, 8):
        for peer in (
            (wide, lax.rem(n + j, NN)),
            (z * NY * NC + lax.rem(plane + j, NY * NC), n),
            (lax.rem(z + j, NZ) * NY * NC + plane, n),
        ):
            pl.semaphore_signal(barrier, inc=1, device_id=peer, device_id_type=MESH)
    load_x.wait()
    load_g.wait()
    pl.semaphore_wait(barrier, 21)

    for j in (2, 1, 3):
        own = xg.at[:, z, c, y]
        remote(own, own, y_send, y_recv, at(z, lax.rem(y + j, NY), c), n).start()

    load_in.wait()
    w_in_h[...], w_in_l[...] = split(w_in_f[...])
    load_out.wait()
    w_out_h[...], w_out_l[...] = split(w_out_f[...].T)
    load_b.wait()

    drain(xg.at[:, z, c, pl.ds(0, 3)], y_recv)
    own = xg.at[:, z, c]
    remote(own, own, c_send, c_recv.at[0], at(z, y, 1 - c), n).start()
    for array in range(2):
        half = xg.at[array, z, c]
        for k in (1, 2):
            to = at(lax.rem(z + (NZ - 1 if k == 2 else 1), NZ), y, c)
            remote(half, half, z_send, z_recv.at[k, array], to, n).start()

    def block_of(k):
        return lax.rem(z + NZ + (1 - 2 * (k % 2)) * ((k + 1) // 2), NZ)

    def arrive(group, array):
        first, count = GROUPS[group]
        for k in range(first, first + count):
            here = xg.at[array, block_of(k), c]
            drain(here, z_recv.at[k, array])
            if k < 5 or k - 5 == array:
                onward = at(lax.rem(z + NZ - 1 + 2 * (k % 2), NZ), y, c)
                remote(here, here, z_send, z_recv.at[k + 2 if k < 5 else 7, array], onward, n).start()
        for k in range(first, first + count):
            here = xg.at[array, block_of(k), c]
            remote(here, here, c_send, c_recv.at[k], at(z, y, 1 - c), n).start()

    def tokens(array, group):
        first, count = GROUPS[group]
        return jnp.concatenate(
            [xg[array, block_of(k)].reshape(BLOCK, FEAT) for k in range(first, first + count)], axis=0
        )

    def hidden(which, group):
        first, count = GROUPS[group]
        return jnp.concatenate(
            [ag[:, k, which].reshape(BLOCK, HID) for k in range(first, first + count)], axis=0
        )

    def forward(group):
        first, count = GROUPS[group]
        for k in range(first, first + count):
            drain(xg.at[:, block_of(k), 1 - c], c_recv.at[k])
        pre = dot3(split(tokens(0, group)), w_in_h[...], w_in_l[...])
        grad_act = dot3(split(tokens(1, group)), w_out_h[...], w_out_l[...])
        for b in range(count):
            rows = slice(b * BLOCK, (b + 1) * BLOCK)
            part[:, first + b, 0] = pre[rows].reshape(NN, ROWS, HID)
            part[:, first + b, 1] = grad_act[rows].reshape(NN, ROWS, HID)
        some = pl.ds(first, count)
        to_right, to_left = yl * NX + right, yl * NX + left
        remote(part.at[far, some], relay.at[0, some], f_send, f_recv.at[group], wide, to_right).start()
        remote(part.at[NX + far, some], relay.at[1, some], f_send, f_recv.at[group], wide, to_left).start()
        remote(part.at[NX + right, some], near.at[0, 1, some], n_send, n_recv.at[group], wide, to_right).start()
        remote(part.at[left, some], near.at[1, 0, some], n_send, n_recv.at[group], wide, to_left).start()

    def keep_tokens(group):
        column, third, start = PLACES[group]
        size = GROUPS[group][1] * BLOCK
        across, along = split(tokens(0, group).T), split(tokens(1, group))
        for i in range(3):
            place = slice(column + third * i + start, column + third * i + start + size)
            x_across[:, place] = across[(0, 1, 0)[i]]
            g_along[place, :] = along[(0, 0, 1)[i]]

    def pass_on(group):
        some = pl.ds(*GROUPS[group])
        drain(relay.at[:, some], f_recv.at[group])
        part[right, some] += relay[0, some]
        part[NX + left, some] += relay[1, some]
        remote(
            part.at[right, some], near.at[0, 0, some], n_send, n_recv.at[group], wide, yl * NX + right
        ).start()
        remote(
            part.at[NX + left, some], near.at[1, 1, some], n_send, n_recv.at[group], wide, yl * NX + left
        ).start()

    def add_x(group):
        some = pl.ds(*GROUPS[group])
        drain(near.at[:, :, some], n_recv.at[group])
        part[over, some] += near[0, 1 - yl, some] + near[1, 1 - yl, some]
        remote(
            part.at[over, some], across_y.at[some], s_y_send, s_y_recv.at[group], wide, over
        ).start()
        part[n, some] += near[0, yl, some] + near[1, yl, some]

    def activate(group):
        some = pl.ds(*GROUPS[group])
        drain(across_y.at[some], s_y_recv.at[group])
        total = part[n, some] + across_y[some]
        act, slope = gelu_parts(total[:, 0] + b_here[...])
        ag[n, some, 0] = act
        ag[n, some, 1] = total[:, 1] * slope
        mine = ag.at[n, some]
        remote(mine, mine, a_send, a_y_recv.at[group], wide, over).start()
        for side in (right, left):
            remote(mine, mine, a_send, a_one_recv.at[group], wide, yl * NX + side).start()

    ahead = lax.rem(x + 1 + 2 * yl, NX)
    behind = lax.rem(x + 3 - 2 * yl, NX)

    def spread(group):
        some = pl.ds(*GROUPS[group])
        drain(across_y.at[some], a_y_recv.at[group])
        other = ag.at[over, some]
        for side in (right, left):
            remote(other, other, a_send, a_two_recv.at[group], wide, yl * NX + side).start()
        drain(ag.at[pl.ds(0, 2), some], a_one_recv.at[group])
        chunk = ag.at[yl * NX + behind, some]
        remote(chunk, chunk, a_send, a_far_recv.at[group], wide, yl * NX + ahead).start()

    def spread_far(group):
        some = pl.ds(*GROUPS[group])
        drain(ag.at[pl.ds(0, 2), some], a_two_recv.at[group])
        chunk = ag.at[(1 - yl) * NX + ahead, some]
        remote(chunk, chunk, a_send, a_far_recv.at[group], wide, yl * NX + behind).start()

    def backward(group):
        first, count = GROUPS[group]
        some = pl.ds(first, count)
        drain(ag.at[pl.ds(0, 2), some], a_far_recv.at[group])
        grad = dot3(split(hidden(1, group)), w_back_h[...], w_back_l[...])
        gi[some] = grad.reshape(count, NC, NY, ROWS, FEAT)
        remote(
            gi.at[some, 1 - c], gi_core.at[some], gc_send, gc_recv.at[group], at(z, y, 1 - c), n
        ).start()

    def keep_hidden(group):
        column, third, start = PLACES[group]
        size = GROUPS[group][1] * BLOCK
        grad_pre = hidden(1, group)
        bias[...] += jnp.sum(grad_pre.reshape(size // 8, 8, HID), axis=0)
        across, along = split(hidden(0, group).T), split(grad_pre)
        for i in range(3):
            place = slice(column + third * i + start, column + third * i + start + size)
            a_across[:, place] = across[(0, 1, 0)[i]]
            p_along[place, :] = along[(0, 0, 1)[i]]

    def hand_over(group):
        first, count = GROUPS[group]
        drain(gi_core.at[pl.ds(first, count)], gc_recv.at[group])
        for k in range(first, first + count):
            gi[k, c] += gi_core[k]
            if 0 < k < FIRST_Y:
                remote(
                    gi.at[k, c], gi_z.at[k - 1], gz_send, gz_recv, at(block_of(k), y, c), n
                ).start()
        if first >= FIRST_Y:
            for j in (2, 1, 3):
                to = lax.rem(y + j, NY)
                remote(
                    gi.at[pl.ds(first, count), c, to],
                    gi_y_first.at[j - 1, pl.ds(first - FIRST_Y, count)],
                    gyf_send, gyf_recv, at(z, to, c), n,
                ).start()

    def to_owner(group):
        first, count = GROUPS[group]
        drain(gi_y_first, gyf_recv)
        for k in range(first, first + count):
            i = k - FIRST_Y
            gi[k, c, y] += gi_y_first[0, i] + (gi_y_first[1, i] + gi_y_first[2, i])
            remote(
                gi.at[k, c, y], gi_z_last.at[i], gzl_send, gzl_recv, at(block_of(k), y, c), n
            ).start()

    def to_vreg(squares):
        rows, columns = squares.shape
        lanes = jnp.sum(squares.reshape(rows // 8, 8, columns), axis=0)
        out = lanes[:, :128]
        for j in range(1, columns // 128):
            out = out + lanes[:, 128 * j:128 * (j + 1)]
        return out

    def weight_round(turn, size, across, along, raw):
        place = slice(ROUNDS[turn][0], sum(ROUNDS[turn]))
        total = jnp.zeros((8, 128), F32)
        for start in range(0, raw.shape[0], size):
            rows = slice(start, start + size)
            tile = product(across[rows, place], along[place, :])
            if turn > 0:
                tile = tile + raw[rows, :]
            if turn == 2:
                total = total + to_vreg(tile * tile)
            raw[rows, :] = tile
        return total

    def weights(turn):
        total = weight_round(turn, 256, x_across, p_along, raw_in_ref)
        return total + weight_round(turn, 128, a_across, g_along, raw_out_ref)

    bias[...] = jnp.zeros_like(bias)
    stages = {
        "h": lambda group: arrive(group, 0), "a": lambda group: arrive(group, 1),
        "0": forward, "1": pass_on, "2": add_x, "3": activate, "4": spread, "5": spread_far,
        "6": backward, "7": hand_over, "x": keep_tokens, "b": keep_hidden, "v": weights,
    }
    forward(0)
    w_back_h[...], w_back_l[...] = split(w_in_f[...].T)
    for order in STEPS:
        for stage, which in zip(order[::2], order[1::2]):
            stages[stage](int(which))
    total = weights(2)

    def share(phase, place, value, peers):
        sums[phase, place] = value
        for peer in peers:
            slot = sums.at[phase, place]
            remote(slot, slot, s_send, s_recv.at[phase], *peer).start()

    def collect(phase):
        drain(sums.at[phase, pl.ds(0, 7)], s_recv.at[phase])
        return jnp.sum(sums[phase], axis=0)

    share(0, n, total, [(wide, lax.rem(n + j, NN)) for j in range(1, 8)])

    hand_over(4)
    total = collect(0)
    share(1, plane, total, [
        (z * NY * NC + lax.rem(plane + j, NY * NC), n) for j in range(1, 8)
    ])
    to_owner(4)
    drain(gi_z, gz_recv)
    own_sum = gi[0, c]
    for j in range(FIRST_Y - 1):
        own_sum = own_sum + gi_z[j]
    gi[0, c] = own_sum
    for j in (2, 1, 3):
        to = lax.rem(y + j, NY)
        remote(gi.at[0, c, to], gi_y.at[j - 1], gy_send, gy_recv, at(z, to, c), n).start()
    bias_in_ref[...] = jnp.sum(bias[...], axis=0, keepdims=True)
    bias_out_ref[...] = jnp.sum(xg[1].reshape(TOKENS, FEAT), axis=0, keepdims=True)
    total = collect(1)
    share(2, z, total, [
        (lax.rem(z + j, NZ) * NY * NC + plane, n) for j in range(1, 8)
    ])
    drain(gi_y, gy_recv)
    drain(gi_z_last, gzl_recv)
    grad_in_ref[...] = ((gi[0, c, y] + gi_y[0]) + (gi_y[1] + gi_y[2])) + gi_z_last[0]
    drain(xg.at[:, z, c, pl.ds(0, 3)], y_send)
    drain(xg.at[:, pl.ds(0, 7), 0], z_send)
    drain(xg.at[:, :, 0], c_send)
    drain(relay, f_send)
    drain(near, n_send)
    drain(across_y, s_y_send)
    drain(ag.at[pl.ds(0, 7)], a_send)
    drain(gi_core, gc_send)
    drain(gi_z, gz_send)
    drain(gi_y, gy_send)
    drain(gi_y_first, gyf_send)
    drain(gi_z_last, gzl_send)
    total = jnp.sum(collect(2), keepdims=True)
    factor = jnp.minimum(1.0, math.sqrt(1.0 * D * FF * TOKENS) / (jnp.sqrt(total) + 1e-06))
    factor_ref[...] = jnp.broadcast_to(factor, factor_ref.shape)
    drain(sums.at[:, pl.ds(0, 7)], s_send)


PIECES = 3


def scale_kernel(
    grad_in_ref, raw_in_ref, raw_out_ref, bias_in_ref, bias_out_ref, factor_ref,
    grad_in_out, gw_in, gw_out, gb_in, gb_out, buf_in, buf_out, sems,
):
    factor = factor_ref[0:1, 0:1]
    stores = []
    for which, (raw, buf, out) in enumerate(
        ((raw_in_ref, buf_in, gw_in), (raw_out_ref, buf_out, gw_out))
    ):
        size = raw.shape[0] // PIECES
        for i in range(PIECES):
            rows = pl.ds(i * size, size)
            buf[rows, :] = raw[rows, :] * factor
            store = pltpu.make_async_copy(buf.at[rows], out.at[rows], sems.at[which, i])
            store.start()
            stores.append(store)
    grad_in_out[...] = grad_in_ref[...]
    gb_in[...] = (bias_in_ref[...] * factor)[0]
    gb_out[...] = (bias_out_ref[...] * factor)[0]
    for store in stores:
        store.wait()


def local(x_tokens, grad_out, w_in, b_in, w_out):
    vmem = pl.BlockSpec(memory_space=pltpu.VMEM)
    anywhere = pl.BlockSpec(memory_space=pl.ANY)
    dma = pltpu.SemaphoreType.DMA
    grad_in, raw_in, raw_out, bias_in, bias_out, factor = pl.pallas_call(
        kernel,
        out_shape=(
            jax.ShapeDtypeStruct((ROWS, FEAT), F32),
            jax.ShapeDtypeStruct((FEAT, HID), F32),
            jax.ShapeDtypeStruct((HID, FEAT), F32),
            jax.ShapeDtypeStruct((1, HID), F32),
            jax.ShapeDtypeStruct((1, FEAT), F32),
            jax.ShapeDtypeStruct((8, 128), F32),
        ),
        in_specs=[pl.BlockSpec(memory_space=pltpu.HBM)] * 5,
        out_specs=(vmem, vmem, vmem, vmem, vmem, vmem),
        scratch_shapes=[
            pltpu.VMEM((2, NZ, NC, NY, ROWS, FEAT), F32),
            pltpu.VMEM((NN, NZ, 2, ROWS, HID), F32),
            pltpu.VMEM((2, NZ, 2, ROWS, HID), F32),
            pltpu.VMEM((2, 2, NZ, 2, ROWS, HID), F32),
            pltpu.VMEM((NZ, 2, ROWS, HID), F32),
            pltpu.VMEM((NN, NZ, 2, ROWS, HID), F32),
            pltpu.VMEM((NZ, NC, NY, ROWS, FEAT), F32),
            pltpu.VMEM((NZ, NY, ROWS, FEAT), F32),
            pltpu.VMEM((FIRST_Y - 1, NY, ROWS, FEAT), F32),
            pltpu.VMEM((NY - 1, ROWS, FEAT), F32),
            pltpu.VMEM((NY - 1, NZ - FIRST_Y, ROWS, FEAT), F32),
            pltpu.VMEM((NZ - FIRST_Y, ROWS, FEAT), F32),
            pltpu.VMEM((3, 8, 8, 128), F32),
            pltpu.VMEM((FEAT, HID), F32),
            pltpu.VMEM((HID, FEAT), F32),
            pltpu.VMEM((FEAT, HID), BF16),
            pltpu.VMEM((FEAT, HID), BF16),
            pltpu.VMEM((FEAT, HID), BF16),
            pltpu.VMEM((FEAT, HID), BF16),
            pltpu.VMEM((HID, FEAT), BF16),
            pltpu.VMEM((HID, FEAT), BF16),
            pltpu.VMEM((FEAT, SUM_COLUMNS), BF16),
            pltpu.VMEM((SUM_COLUMNS, FEAT), BF16),
            pltpu.VMEM((SUM_COLUMNS, HID), BF16),
            pltpu.VMEM((HID, SUM_COLUMNS), BF16),
            pltpu.VMEM((ROWS, HID), F32),
            pltpu.VMEM((HID,), F32),
            dma((5,)),
            dma, dma,
            dma, dma((NZ, 2)),
            dma, dma((NZ,)),
            dma, dma((5,)),
            dma, dma((5,)),
            dma, dma((5,)),
            dma, dma((5,)), dma((5,)), dma((5,)), dma((5,)),
            dma, dma((5,)),
            dma, dma,
            dma, dma,
            dma, dma,
            dma, dma,
            dma, dma((3,)),
        ],
        compiler_params=pltpu.CompilerParams(
            collective_id=0, has_side_effects=True, vmem_limit_bytes=51 * 1024 * 1024
        ),
    )(x_tokens, grad_out, w_in, b_in, w_out)
    return pl.pallas_call(
        scale_kernel,
        out_shape=(
            jax.ShapeDtypeStruct((ROWS, FEAT), F32),
            jax.ShapeDtypeStruct((FEAT, HID), F32),
            jax.ShapeDtypeStruct((HID, FEAT), F32),
            jax.ShapeDtypeStruct((HID,), F32),
            jax.ShapeDtypeStruct((FEAT,), F32),
        ),
        in_specs=[vmem, vmem, vmem, vmem, vmem, vmem],
        out_specs=(vmem, anywhere, anywhere, vmem, vmem),
        scratch_shapes=[
            pltpu.VMEM((FEAT, HID), F32),
            pltpu.VMEM((HID, FEAT), F32),
            dma((2, PIECES)),
        ],
        compiler_params=pltpu.CompilerParams(vmem_limit_bytes=16 * 1024 * 1024),
    )(grad_in, raw_in, raw_out, bias_in, bias_out, factor)


def solution(mesh):
    placed = (
        P("wide", "narrow"),
        P("wide", "narrow"),
        P("narrow", "wide"),
        P("wide"),
        P("wide", "narrow"),
    )
    return jax.shard_map(
        local,
        mesh=mesh,
        in_specs=placed,
        out_specs=(
            P("wide", "narrow"),
            P("narrow", "wide"),
            P("wide", "narrow"),
            P("wide"),
            P("narrow"),
        ),
        check_vma=False,
    )
```

```python
import math

import jax
import jax.numpy as jnp
from jax import lax
from jax.experimental import pallas as pl
from jax.experimental.pallas import tpu as pltpu
from jax.sharding import PartitionSpec as P

D = 6144
FF = 24576
TOKENS = 512
MESH = pl.DeviceIdType.MESH
F32, BF16 = jnp.float32, jnp.bfloat16

NZ, NY, NC, NN = 8, 4, 2, 8
ROWS = 8
BLOCK = NY * NC * ROWS
NX = 4
GROUPS = ((0, 1), (1, 2), (3, 2), (5, 2), (7, 1))
PLACES = ((1152, 128, 0), (0, 256, 0), (0, 256, 128), (768, 128, 0), (1152, 128, 64))
ROUNDS = ((0, 768), (768, 384), (1152, 384))
SUM_COLUMNS = 1536
FIRST_Y = 7
STEPS = (
    "x0h1a11001x1h230a211h30240x231a3h41203a460b0x3410470",
    "32x41361b1147142333462b2v043724463b3v17364b4",
)
FEAT, HID = 768, 384

tanh_scale = math.sqrt(2.0 / math.pi)
cubic_weight = 0.044715


def gelu_parts(pre):
    inner = tanh_scale * (pre + cubic_weight * pre * pre * pre)
    tangent = jnp.tanh(inner)
    value = 0.5 * pre * (1.0 + tangent)
    slope = 0.5 * (1.0 + tangent) + 0.5 * pre * (1.0 - tangent * tangent) * tanh_scale * (
        1.0 + 3.0 * cubic_weight * pre * pre
    )
    return (value, slope)


def split(values):
    high = values.astype(BF16)
    return high, (values - high.astype(F32)).astype(BF16)


def product(left, right):
    return jnp.dot(left, right, preferred_element_type=F32)


def dot3(pair, high, low):
    rows = pair[0].shape[0]
    both = product(jnp.concatenate(pair, axis=0), high)
    return (both[:rows] + both[rows:]) + product(pair[0], low)


def remote(source, target, send, recv, wide, narrow):
    return pltpu.make_async_remote_copy(
        src_ref=source,
        dst_ref=target,
        send_sem=send,
        recv_sem=recv,
        device_id=(wide, narrow),
        device_id_type=MESH,
    )


def drain(ref, sem):
    pltpu.make_async_copy(ref, ref, sem).wait()


def kernel(
    x_ref, g_ref, w_in_ref, b_ref, w_out_ref,
    grad_in_ref, raw_in_ref, raw_out_ref, bias_in_ref, bias_out_ref, factor_ref,
    xg, part, relay, near, ag, gi, gi_core, gi_z, gi_y, gi_y_first, gi_z_last, sums,
    w_in_f, w_out_f, w_in_h, w_in_l, w_out_h, w_out_l, w_back_h, w_back_l,
    x_across, g_along, p_along, a_across, bias, b_here,
    load_sem, y_send, y_recv, z_send, z_recv, c_send, c_recv,
    f_send, f_recv, n_send, n_recv, a_send, a_one_recv, a_far_recv,
    gc_send, gc_recv, gz_send, gz_recv, gy_send, gy_recv, gyf_send, gyf_recv, gzl_send, gzl_recv,
    s_send, s_recv,
):
    wide = lax.axis_index("wide")
    n = lax.axis_index("narrow")
    z = lax.div(wide, NY * NC)
    y = lax.rem(lax.div(wide, NC), NY)
    c = lax.rem(wide, NC)

    yl = lax.div(n, NX)
    x = lax.rem(n, NX)
    right, left, far = (lax.rem(x + j, NX) for j in (1, 3, 2))
    over = (1 - yl) * NX + x

    def at(zz, yy, cc):
        return (zz * NY + yy) * NC + cc

    load_in = pltpu.make_async_copy(w_in_ref, w_in_f, load_sem.at[0])
    load_out = pltpu.make_async_copy(w_out_ref, w_out_f, load_sem.at[1])
    load_x = pltpu.make_async_copy(x_ref, xg.at[0, z, c, y], load_sem.at[2])
    load_g = pltpu.make_async_copy(g_ref, xg.at[1, z, c, y], load_sem.at[3])
    load_b = pltpu.make_async_copy(b_ref, b_here, load_sem.at[4])
    for load in (load_x, load_g, load_in, load_out, load_b):
        load.start()

    plane = lax.rem(wide, NY * NC)
    barrier = pltpu.get_barrier_semaphore()
    for j in range(1, 8):
        for peer in (
            (wide, lax.rem(n + j, NN)),
            (z * NY * NC + lax.rem(plane + j, NY * NC), n),
            (lax.rem(z + j, NZ) * NY * NC + plane, n),
        ):
            pl.semaphore_signal(barrier, inc=1, device_id=peer, device_id_type=MESH)
    load_x.wait()
    load_g.wait()
    pl.semaphore_wait(barrier, 21)

    def first_row(row):
        part_of = xg.at[:, z, c, row]
        for k in (1, 2):
            to = at(lax.rem(z + (NZ - 1 if k == 2 else 1), NZ), y, c)
            remote(part_of, part_of, z_send, z_recv.at[k, 0], to, n).start()
        remote(part_of, part_of, c_send, c_recv.at[0], at(z, y, 1 - c), n).start()

    def next_row(j):
        row = lax.rem(y + NY - j, NY)
        drain(xg.at[:, z, c, row], y_recv.at[j - 1])
        first_row(row)

    own = xg.at[:, z, c, y]
    for j in (1, 3, 2):
        remote(own, own, y_send, y_recv.at[j - 1], at(z, lax.rem(y + j, NY), c), n).start()
    first_row(y)
    load_in.wait()
    w_in_h[...], w_in_l[...] = split(w_in_f[...])
    next_row(1)
    next_row(3)
    load_out.wait()
    w_out_h[...], w_out_l[...] = split(w_out_f[...].T)
    load_b.wait()
    next_row(2)

    def block_of(k):
        return lax.rem(z + NZ + (1 - 2 * (k % 2)) * ((k + 1) // 2), NZ)

    def arrive(group, array):
        first, count = GROUPS[group]
        for k in range(first, first + count):
            here = xg.at[array, block_of(k), c]
            if group > 1:
                drain(here, z_recv.at[k, array])
            elif array == 0:
                drain(xg.at[:, block_of(k), c], z_recv.at[k, 0])
            if k < 5 or k - 5 == array:
                onward = at(lax.rem(z + NZ - 1 + 2 * (k % 2), NZ), y, c)
                remote(here, here, z_send, z_recv.at[k + 2 if k < 5 else 7, array], onward, n).start()
        for k in range(first, first + count):
            here = xg.at[array, block_of(k), c]
            remote(here, here, c_send, c_recv.at[k], at(z, y, 1 - c), n).start()

    def tokens(array, group):
        first, count = GROUPS[group]
        return jnp.concatenate(
            [xg[array, block_of(k)].reshape(BLOCK, FEAT) for k in range(first, first + count)], axis=0
        )

    def hidden(which, group):
        first, count = GROUPS[group]
        return jnp.concatenate(
            [ag[:, k, which].reshape(BLOCK, HID) for k in range(first, first + count)], axis=0
        )

    def forward(group):
        first, count = GROUPS[group]
        for k in range(first, first + count):
            drain(xg.at[:, block_of(k), 1 - c], c_recv.at[k])
        pre = dot3(split(tokens(0, group)), w_in_h[...], w_in_l[...])
        grad_act = dot3(split(tokens(1, group)), w_out_h[...], w_out_l[...])
        for b in range(count):
            rows = slice(b * BLOCK, (b + 1) * BLOCK)
            part[:, first + b, 0] = pre[rows].reshape(NN, ROWS, HID)
            part[:, first + b, 1] = grad_act[rows].reshape(NN, ROWS, HID)
        some = pl.ds(first, count)
        to_right, to_left = yl * NX + right, yl * NX + left
        remote(part.at[far, some], relay.at[0, some], f_send, f_recv.at[group], wide, to_right).start()
        remote(part.at[NX + far, some], relay.at[1, some], f_send, f_recv.at[group], wide, to_left).start()
        for owner, slot in ((NX + right, 3 - 2 * yl), (left, 2 + 2 * yl), (over, 0)):
            remote(part.at[owner, some], near.at[slot, some], n_send, n_recv.at[group], wide, owner).start()

    def keep_tokens(group):
        column, third, start = PLACES[group]
        size = GROUPS[group][1] * BLOCK
        across, along = split(tokens(0, group).T), split(tokens(1, group))
        for i in range(3):
            place = slice(column + third * i + start, column + third * i + start + size)
            x_across[:, place] = across[(0, 1, 0)[i]]
            g_along[place, :] = along[(0, 0, 1)[i]]

    def pass_on(group):
        some = pl.ds(*GROUPS[group])
        drain(relay.at[:, some], f_recv.at[group])
        part[right, some] += relay[0, some]
        part[NX + left, some] += relay[1, some]
        for owner, slot in ((right, 1 + 2 * yl), (NX + left, 4 - 2 * yl)):
            remote(part.at[owner, some], near.at[slot, some], n_send, n_recv.at[group], wide, owner).start()

    def activate(group):
        some = pl.ds(*GROUPS[group])
        drain(near.at[:, some], n_recv.at[group])
        total = part[n, some]
        for j in range(5):
            total = total + near[j, some]
        act, slope = gelu_parts(total[:, 0] + b_here[...])
        ag[n, some, 0] = act
        ag[n, some, 1] = total[:, 1] * slope
        mine = ag.at[n, some]
        for peer in (right, NX + right, left, NX + left, over):
            remote(mine, mine, a_send, a_one_recv.at[group], wide, peer).start()

    def spread(group):
        some = pl.ds(*GROUPS[group])
        drain(ag.at[pl.ds(0, 5), some], a_one_recv.at[group])
        for owner, peer in ((left, yl * NX + right), (NX + right, yl * NX + left)):
            chunk = ag.at[owner, some]
            remote(chunk, chunk, a_send, a_far_recv.at[group], wide, peer).start()

    def backward(group):
        first, count = GROUPS[group]
        some = pl.ds(first, count)
        drain(ag.at[pl.ds(0, 2), some], a_far_recv.at[group])
        grad = dot3(split(hidden(1, group)), w_back_h[...], w_back_l[...])
        gi[some] = grad.reshape(count, NC, NY, ROWS, FEAT)
        remote(
            gi.at[some, 1 - c], gi_core.at[some], gc_send, gc_recv.at[group], at(z, y, 1 - c), n
        ).start()

    def keep_hidden(group):
        column, third, start = PLACES[group]
        size = GROUPS[group][1] * BLOCK
        grad_pre = hidden(1, group)
        bias[...] += jnp.sum(grad_pre.reshape(size // 8, 8, HID), axis=0)
        across, along = split(hidden(0, group).T), split(grad_pre)
        for i in range(3):
            place = slice(column + third * i + start, column + third * i + start + size)
            a_across[:, place] = across[(0, 1, 0)[i]]
            p_along[place, :] = along[(0, 0, 1)[i]]

    def hand_over(group):
        first, count = GROUPS[group]
        drain(gi_core.at[pl.ds(first, count)], gc_recv.at[group])
        for k in range(first, first + count):
            gi[k, c] += gi_core[k]
            if 0 < k < FIRST_Y:
                remote(
                    gi.at[k, c], gi_z.at[k - 1], gz_send, gz_recv, at(block_of(k), y, c), n
                ).start()
        if first >= FIRST_Y:
            for j in (2, 1, 3):
                to = lax.rem(y + j, NY)
                remote(
                    gi.at[pl.ds(first, count), c, to],
                    gi_y_first.at[j - 1, pl.ds(first - FIRST_Y, count)],
                    gyf_send, gyf_recv, at(z, to, c), n,
                ).start()

    def to_owner(group):
        first, count = GROUPS[group]
        drain(gi_y_first, gyf_recv)
        for k in range(first, first + count):
            i = k - FIRST_Y
            gi[k, c, y] += gi_y_first[0, i] + (gi_y_first[1, i] + gi_y_first[2, i])
            remote(
                gi.at[k, c, y], gi_z_last.at[i], gzl_send, gzl_recv, at(block_of(k), y, c), n
            ).start()

    def to_vreg(squares):
        rows, columns = squares.shape
        lanes = jnp.sum(squares.reshape(rows // 8, 8, columns), axis=0)
        out = lanes[:, :128]
        for j in range(1, columns // 128):
            out = out + lanes[:, 128 * j:128 * (j + 1)]
        return out

    def weight_round(turn, size, across, along, raw):
        place = slice(ROUNDS[turn][0], sum(ROUNDS[turn]))
        total = jnp.zeros((8, 128), F32)
        for start in range(0, raw.shape[0], size):
            rows = slice(start, start + size)
            tile = product(across[rows, place], along[place, :])
            if turn > 0:
                tile = tile + raw[rows, :]
            if turn == 2:
                total = total + to_vreg(tile * tile)
            raw[rows, :] = tile
        return total

    def weights(turn):
        total = weight_round(turn, 256, x_across, p_along, raw_in_ref)
        return total + weight_round(turn, 128, a_across, g_along, raw_out_ref)

    bias[...] = jnp.zeros_like(bias)
    stages = {
        "h": lambda group: arrive(group, 0), "a": lambda group: arrive(group, 1),
        "0": forward, "1": pass_on, "3": activate, "4": spread,
        "6": backward, "7": hand_over, "x": keep_tokens, "b": keep_hidden, "v": weights,
    }
    forward(0)
    w_back_h[...], w_back_l[...] = split(w_in_f[...].T)
    for order in STEPS:
        for stage, which in zip(order[::2], order[1::2]):
            stages[stage](int(which))
    total = weights(2)

    def share(phase, place, value, peers):
        sums[phase, place] = value
        for peer in peers:
            slot = sums.at[phase, place]
            remote(slot, slot, s_send, s_recv.at[phase], *peer).start()

    def collect(phase):
        drain(sums.at[phase, pl.ds(0, 7)], s_recv.at[phase])
        return jnp.sum(sums[phase], axis=0)

    share(0, n, total, [(wide, lax.rem(n + j, NN)) for j in range(1, 8)])

    hand_over(4)
    total = collect(0)
    share(1, plane, total, [
        (z * NY * NC + lax.rem(plane + j, NY * NC), n) for j in range(1, 8)
    ])
    to_owner(4)
    drain(gi_z, gz_recv)
    own_sum = gi[0, c]
    for j in range(FIRST_Y - 1):
        own_sum = own_sum + gi_z[j]
    gi[0, c] = own_sum
    for j in (2, 1, 3):
        to = lax.rem(y + j, NY)
        remote(gi.at[0, c, to], gi_y.at[j - 1], gy_send, gy_recv, at(z, to, c), n).start()
    bias_in_ref[...] = jnp.sum(bias[...], axis=0, keepdims=True)
    bias_out_ref[...] = jnp.sum(xg[1].reshape(TOKENS, FEAT), axis=0, keepdims=True)
    total = collect(1)
    share(2, z, total, [
        (lax.rem(z + j, NZ) * NY * NC + plane, n) for j in range(1, 8)
    ])
    drain(gi_y, gy_recv)
    drain(gi_z_last, gzl_recv)
    grad_in_ref[...] = ((gi[0, c, y] + gi_y[0]) + (gi_y[1] + gi_y[2])) + gi_z_last[0]
    drain(xg.at[:, z, c, pl.ds(0, 3)], y_send)
    drain(xg.at[:, pl.ds(0, 7), 0], z_send)
    drain(xg.at[:, :, 0], c_send)
    drain(relay, f_send)
    drain(near, n_send)
    drain(ag.at[pl.ds(0, 7)], a_send)
    drain(gi_core, gc_send)
    drain(gi_z, gz_send)
    drain(gi_y, gy_send)
    drain(gi_y_first, gyf_send)
    drain(gi_z_last, gzl_send)
    total = jnp.sum(collect(2), keepdims=True)
    factor = jnp.minimum(1.0, math.sqrt(1.0 * D * FF * TOKENS) / (jnp.sqrt(total) + 1e-06))
    factor_ref[...] = jnp.broadcast_to(factor, factor_ref.shape)
    drain(sums.at[:, pl.ds(0, 7)], s_send)


PIECES = 3


def scale_kernel(
    grad_in_ref, raw_in_ref, raw_out_ref, bias_in_ref, bias_out_ref, factor_ref,
    grad_in_out, gw_in, gw_out, gb_in, gb_out, buf_in, buf_out, sems,
):
    factor = factor_ref[0:1, 0:1]
    stores = []
    for which, (raw, buf, out) in enumerate(
        ((raw_in_ref, buf_in, gw_in), (raw_out_ref, buf_out, gw_out))
    ):
        size = raw.shape[0] // PIECES
        for i in range(PIECES):
            rows = pl.ds(i * size, size)
            buf[rows, :] = raw[rows, :] * factor
            store = pltpu.make_async_copy(buf.at[rows], out.at[rows], sems.at[which, i])
            store.start()
            stores.append(store)
    grad_in_out[...] = grad_in_ref[...]
    gb_in[...] = (bias_in_ref[...] * factor)[0]
    gb_out[...] = (bias_out_ref[...] * factor)[0]
    for store in stores:
        store.wait()


def local(x_tokens, grad_out, w_in, b_in, w_out):
    vmem = pl.BlockSpec(memory_space=pltpu.VMEM)
    anywhere = pl.BlockSpec(memory_space=pl.ANY)
    dma = pltpu.SemaphoreType.DMA
    grad_in, raw_in, raw_out, bias_in, bias_out, factor = pl.pallas_call(
        kernel,
        out_shape=(
            jax.ShapeDtypeStruct((ROWS, FEAT), F32),
            jax.ShapeDtypeStruct((FEAT, HID), F32),
            jax.ShapeDtypeStruct((HID, FEAT), F32),
            jax.ShapeDtypeStruct((1, HID), F32),
            jax.ShapeDtypeStruct((1, FEAT), F32),
            jax.ShapeDtypeStruct((8, 128), F32),
        ),
        in_specs=[pl.BlockSpec(memory_space=pltpu.HBM)] * 5,
        out_specs=(vmem, vmem, vmem, vmem, vmem, vmem),
        scratch_shapes=[
            pltpu.VMEM((2, NZ, NC, NY, ROWS, FEAT), F32),
            pltpu.VMEM((NN, NZ, 2, ROWS, HID), F32),
            pltpu.VMEM((2, NZ, 2, ROWS, HID), F32),
            pltpu.VMEM((5, NZ, 2, ROWS, HID), F32),
            pltpu.VMEM((NN, NZ, 2, ROWS, HID), F32),
            pltpu.VMEM((NZ, NC, NY, ROWS, FEAT), F32),
            pltpu.VMEM((NZ, NY, ROWS, FEAT), F32),
            pltpu.VMEM((FIRST_Y - 1, NY, ROWS, FEAT), F32),
            pltpu.VMEM((NY - 1, ROWS, FEAT), F32),
            pltpu.VMEM((NY - 1, NZ - FIRST_Y, ROWS, FEAT), F32),
            pltpu.VMEM((NZ - FIRST_Y, ROWS, FEAT), F32),
            pltpu.VMEM((3, 8, 8, 128), F32),
            pltpu.VMEM((FEAT, HID), F32),
            pltpu.VMEM((HID, FEAT), F32),
            pltpu.VMEM((FEAT, HID), BF16),
            pltpu.VMEM((FEAT, HID), BF16),
            pltpu.VMEM((FEAT, HID), BF16),
            pltpu.VMEM((FEAT, HID), BF16),
            pltpu.VMEM((HID, FEAT), BF16),
            pltpu.VMEM((HID, FEAT), BF16),
            pltpu.VMEM((FEAT, SUM_COLUMNS), BF16),
            pltpu.VMEM((SUM_COLUMNS, FEAT), BF16),
            pltpu.VMEM((SUM_COLUMNS, HID), BF16),
            pltpu.VMEM((HID, SUM_COLUMNS), BF16),
            pltpu.VMEM((ROWS, HID), F32),
            pltpu.VMEM((HID,), F32),
            dma((5,)),
            dma, dma((NY - 1,)),
            dma, dma((NZ, 2)),
            dma, dma((NZ,)),
            dma, dma((5,)),
            dma, dma((5,)),
            dma, dma((5,)), dma((5,)),
            dma, dma((5,)),
            dma, dma,
            dma, dma,
            dma, dma,
            dma, dma,
            dma, dma((3,)),
        ],
        compiler_params=pltpu.CompilerParams(
            collective_id=0, has_side_effects=True, vmem_limit_bytes=51 * 1024 * 1024
        ),
    )(x_tokens, grad_out, w_in, b_in, w_out)
    return pl.pallas_call(
        scale_kernel,
        out_shape=(
            jax.ShapeDtypeStruct((ROWS, FEAT), F32),
            jax.ShapeDtypeStruct((FEAT, HID), F32),
            jax.ShapeDtypeStruct((HID, FEAT), F32),
            jax.ShapeDtypeStruct((HID,), F32),
            jax.ShapeDtypeStruct((FEAT,), F32),
        ),
        in_specs=[vmem, vmem, vmem, vmem, vmem, vmem],
        out_specs=(vmem, anywhere, anywhere, vmem, vmem),
        scratch_shapes=[
            pltpu.VMEM((FEAT, HID), F32),
            pltpu.VMEM((HID, FEAT), F32),
            dma((2, PIECES)),
        ],
        compiler_params=pltpu.CompilerParams(vmem_limit_bytes=16 * 1024 * 1024),
    )(grad_in, raw_in, raw_out, bias_in, bias_out, factor)


def solution(mesh):
    placed = (
        P("wide", "narrow"),
        P("wide", "narrow"),
        P("narrow", "wide"),
        P("wide"),
        P("wide", "narrow"),
    )
    return jax.shard_map(
        local,
        mesh=mesh,
        in_specs=placed,
        out_specs=(
            P("wide", "narrow"),
            P("narrow", "wide"),
            P("wide", "narrow"),
            P("wide"),
            P("narrow"),
        ),
        check_vma=False,
    )
```

```python
import math

import jax
import jax.numpy as jnp
from jax import lax
from jax.experimental import pallas as pl
from jax.experimental.pallas import tpu as pltpu
from jax.sharding import PartitionSpec as P

D = 6144
FF = 24576
TOKENS = 512
MESH = pl.DeviceIdType.MESH
F32, BF16 = jnp.float32, jnp.bfloat16

NZ, NY, NC, NN = 8, 4, 2, 8
ROWS = 8
BLOCK = NY * NC * ROWS
NX = 4
GROUPS = ((0, 1), (1, 2), (3, 2), (5, 2), (7, 1))
PLACES = ((1152, 128, 0), (0, 256, 0), (0, 256, 128), (768, 128, 0), (1152, 128, 64))
ROUNDS = ((0, 768), (768, 384), (1152, 384))
SUM_COLUMNS = 1536
FIRST_Y = 5
STEPS = (
    "x0h1a11001x1h230a211h30240x231a3h41203a460x3b0410470",
    "x413326114b1337142346243b2v044v17263b364w0w173b474u0u1",
)
FEAT, HID = 768, 384

tanh_scale = math.sqrt(2.0 / math.pi)
cubic_weight = 0.044715


def gelu_parts(pre):
    inner = tanh_scale * (pre + cubic_weight * pre * pre * pre)
    tangent = jnp.tanh(inner)
    value = 0.5 * pre * (1.0 + tangent)
    slope = 0.5 * (1.0 + tangent) + 0.5 * pre * (1.0 - tangent * tangent) * tanh_scale * (
        1.0 + 3.0 * cubic_weight * pre * pre
    )
    return (value, slope)


def split(values):
    high = values.astype(BF16)
    return high, (values - high.astype(F32)).astype(BF16)


def product(left, right):
    return jnp.dot(left, right, preferred_element_type=F32)


def dot3(pair, high, low):
    rows = pair[0].shape[0]
    both = product(jnp.concatenate(pair, axis=0), high)
    return (both[:rows] + both[rows:]) + product(pair[0], low)


def remote(source, target, send, recv, wide, narrow):
    return pltpu.make_async_remote_copy(
        src_ref=source,
        dst_ref=target,
        send_sem=send,
        recv_sem=recv,
        device_id=(wide, narrow),
        device_id_type=MESH,
    )


def drain(ref, sem):
    pltpu.make_async_copy(ref, ref, sem).wait()


def kernel(
    x_ref, g_ref, w_in_ref, b_ref, w_out_ref,
    grad_in_ref, raw_in_ref, raw_out_ref, bias_in_ref, bias_out_ref, factor_ref,
    xg, part, relay, near, ag, gi, gi_core, gi_z, gi_y, gi_y_first, gi_z_last, sums,
    w_in_f, w_out_f, w_in_h, w_in_l, w_out_h, w_out_l, w_back_h, w_back_l,
    x_across, g_along, p_along, a_across, bias, b_here,
    load_sem, y_send, y_recv, z_send, z_recv, c_send, c_recv,
    f_send, f_recv, n_send, n_recv, a_send, a_one_recv, a_far_recv,
    gc_send, gc_recv, gz_send, gz_recv, gy_send, gy_recv, gyf_send, gyf_recv, gzl_send, gzl_recv,
    s_send, s_recv,
):
    wide = lax.axis_index("wide")
    n = lax.axis_index("narrow")
    z = lax.div(wide, NY * NC)
    y = lax.rem(lax.div(wide, NC), NY)
    c = lax.rem(wide, NC)

    yl = lax.div(n, NX)
    x = lax.rem(n, NX)
    right, left, far = (lax.rem(x + j, NX) for j in (1, 3, 2))
    over = (1 - yl) * NX + x

    def at(zz, yy, cc):
        return (zz * NY + yy) * NC + cc

    load_in = pltpu.make_async_copy(w_in_ref, w_in_f, load_sem.at[0])
    load_out = pltpu.make_async_copy(w_out_ref, w_out_f, load_sem.at[1])
    load_x = pltpu.make_async_copy(x_ref, xg.at[0, z, c, y], load_sem.at[2])
    load_g = pltpu.make_async_copy(g_ref, xg.at[1, z, c, y], load_sem.at[3])
    load_b = pltpu.make_async_copy(b_ref, b_here, load_sem.at[4])
    for load in (load_x, load_g, load_in, load_out, load_b):
        load.start()

    plane = lax.rem(wide, NY * NC)
    barrier = pltpu.get_barrier_semaphore()
    for j in range(1, 8):
        for peer in (
            (wide, lax.rem(n + j, NN)),
            (z * NY * NC + lax.rem(plane + j, NY * NC), n),
            (lax.rem(z + j, NZ) * NY * NC + plane, n),
        ):
            pl.semaphore_signal(barrier, inc=1, device_id=peer, device_id_type=MESH)
    load_x.wait()
    load_g.wait()
    pl.semaphore_wait(barrier, 21)

    def first_row(row):
        part_of = xg.at[:, z, c, row]
        for k in (1, 2):
            to = at(lax.rem(z + (NZ - 1 if k == 2 else 1), NZ), y, c)
            remote(part_of, part_of, z_send, z_recv.at[k, 0], to, n).start()
        remote(part_of, part_of, c_send, c_recv.at[0], at(z, y, 1 - c), n).start()

    def next_row(j):
        row = lax.rem(y + NY - j, NY)
        drain(xg.at[:, z, c, row], y_recv.at[j - 1])
        first_row(row)

    own = xg.at[:, z, c, y]
    for j in (1, 3, 2):
        remote(own, own, y_send, y_recv.at[j - 1], at(z, lax.rem(y + j, NY), c), n).start()
    first_row(y)
    load_in.wait()
    w_in_h[...], w_in_l[...] = split(w_in_f[...])
    next_row(1)
    next_row(3)
    load_out.wait()
    w_out_h[...], w_out_l[...] = split(w_out_f[...].T)
    load_b.wait()
    next_row(2)

    def block_of(k):
        return lax.rem(z + NZ + (1 - 2 * (k % 2)) * ((k + 1) // 2), NZ)

    def arrive(group, array):
        first, count = GROUPS[group]
        for k in range(first, first + count):
            here = xg.at[array, block_of(k), c]
            if group > 1:
                drain(here, z_recv.at[k, array])
            elif array == 0:
                drain(xg.at[:, block_of(k), c], z_recv.at[k, 0])
            if k < 5 or k - 5 == array:
                onward = at(lax.rem(z + NZ - 1 + 2 * (k % 2), NZ), y, c)
                remote(here, here, z_send, z_recv.at[k + 2 if k < 5 else 7, array], onward, n).start()
        for k in range(first, first + count):
            here = xg.at[array, block_of(k), c]
            remote(here, here, c_send, c_recv.at[k], at(z, y, 1 - c), n).start()

    def tokens(array, group):
        first, count = GROUPS[group]
        return jnp.concatenate(
            [xg[array, block_of(k)].reshape(BLOCK, FEAT) for k in range(first, first + count)], axis=0
        )

    def hidden(which, group):
        first, count = GROUPS[group]
        return jnp.concatenate(
            [ag[:, k, which].reshape(BLOCK, HID) for k in range(first, first + count)], axis=0
        )

    def forward(group):
        first, count = GROUPS[group]
        for k in range(first, first + count):
            drain(xg.at[:, block_of(k), 1 - c], c_recv.at[k])
        pre = dot3(split(tokens(0, group)), w_in_h[...], w_in_l[...])
        grad_act = dot3(split(tokens(1, group)), w_out_h[...], w_out_l[...])
        for b in range(count):
            rows = slice(b * BLOCK, (b + 1) * BLOCK)
            part[:, first + b, 0] = pre[rows].reshape(NN, ROWS, HID)
            part[:, first + b, 1] = grad_act[rows].reshape(NN, ROWS, HID)
        some = pl.ds(first, count)
        to_right, to_left = yl * NX + right, yl * NX + left
        remote(part.at[far, some], relay.at[0, some], f_send, f_recv.at[group], wide, to_right).start()
        remote(part.at[NX + far, some], relay.at[1, some], f_send, f_recv.at[group], wide, to_left).start()
        for owner, slot in ((NX + right, 3 - 2 * yl), (left, 2 + 2 * yl), (over, 0)):
            remote(part.at[owner, some], near.at[slot, some], n_send, n_recv.at[group], wide, owner).start()

    def keep_tokens(group):
        column, third, start = PLACES[group]
        size = GROUPS[group][1] * BLOCK
        across, along = split(tokens(0, group).T), split(tokens(1, group))
        for i in range(3):
            place = slice(column + third * i + start, column + third * i + start + size)
            x_across[:, place] = across[(0, 1, 0)[i]]
            g_along[place, :] = along[(0, 0, 1)[i]]

    def pass_on(group):
        some = pl.ds(*GROUPS[group])
        drain(relay.at[:, some], f_recv.at[group])
        part[right, some] += relay[0, some]
        part[NX + left, some] += relay[1, some]
        for owner, slot in ((right, 1 + 2 * yl), (NX + left, 4 - 2 * yl)):
            remote(part.at[owner, some], near.at[slot, some], n_send, n_recv.at[group], wide, owner).start()

    def activate(group):
        some = pl.ds(*GROUPS[group])
        drain(near.at[:, some], n_recv.at[group])
        total = part[n, some]
        for j in range(5):
            total = total + near[j, some]
        act, slope = gelu_parts(total[:, 0] + b_here[...])
        ag[n, some, 0] = act
        ag[n, some, 1] = total[:, 1] * slope
        mine = ag.at[n, some]
        for peer in (right, NX + right, left, NX + left, over):
            remote(mine, mine, a_send, a_one_recv.at[group], wide, peer).start()

    def spread(group):
        some = pl.ds(*GROUPS[group])
        drain(ag.at[pl.ds(0, 5), some], a_one_recv.at[group])
        for owner, peer in ((left, yl * NX + right), (NX + right, yl * NX + left)):
            chunk = ag.at[owner, some]
            remote(chunk, chunk, a_send, a_far_recv.at[group], wide, peer).start()

    def backward(group):
        first, count = GROUPS[group]
        some = pl.ds(first, count)
        drain(ag.at[pl.ds(0, 2), some], a_far_recv.at[group])
        grad = dot3(split(hidden(1, group)), w_back_h[...], w_back_l[...])
        gi[some] = grad.reshape(count, NC, NY, ROWS, FEAT)
        remote(
            gi.at[some, 1 - c], gi_core.at[some], gc_send, gc_recv.at[group], at(z, y, 1 - c), n
        ).start()

    def keep_hidden(group):
        column, third, start = PLACES[group]
        size = GROUPS[group][1] * BLOCK
        grad_pre = hidden(1, group)
        bias[...] += jnp.sum(grad_pre.reshape(size // 8, 8, HID), axis=0)
        across, along = split(hidden(0, group).T), split(grad_pre)
        for i in range(3):
            place = slice(column + third * i + start, column + third * i + start + size)
            a_across[:, place] = across[(0, 1, 0)[i]]
            p_along[place, :] = along[(0, 0, 1)[i]]

    def hand_over(group):
        first, count = GROUPS[group]
        drain(gi_core.at[pl.ds(first, count)], gc_recv.at[group])
        for k in range(first, first + count):
            gi[k, c] += gi_core[k]
            if 0 < k < FIRST_Y:
                remote(
                    gi.at[k, c], gi_z.at[k - 1], gz_send, gz_recv, at(block_of(k), y, c), n
                ).start()
        if first >= FIRST_Y:
            for j in (2, 1, 3):
                to = lax.rem(y + j, NY)
                remote(
                    gi.at[pl.ds(first, count), c, to],
                    gi_y_first.at[j - 1, pl.ds(first - FIRST_Y, count)],
                    gyf_send, gyf_recv.at[group - 3], at(z, to, c), n,
                ).start()

    def to_owner(group):
        first, count = GROUPS[group]
        drain(gi_y_first.at[:, pl.ds(first - FIRST_Y, count)], gyf_recv.at[group - 3])
        for k in range(first, first + count):
            i = k - FIRST_Y
            gi[k, c, y] += gi_y_first[0, i] + (gi_y_first[1, i] + gi_y_first[2, i])
            remote(
                gi.at[k, c, y], gi_z_last.at[i], gzl_send, gzl_recv, at(block_of(k), y, c), n
            ).start()

    def to_vreg(squares):
        rows, columns = squares.shape
        lanes = jnp.sum(squares.reshape(rows // 8, 8, columns), axis=0)
        out = lanes[:, :128]
        for j in range(1, columns // 128):
            out = out + lanes[:, 128 * j:128 * (j + 1)]
        return out

    def weight_round(turn, size, across, along, raw):
        place = slice(ROUNDS[turn][0], sum(ROUNDS[turn]))
        total = jnp.zeros((8, 128), F32)
        for start in range(0, raw.shape[0], size):
            rows = slice(start, start + size)
            tile = product(across[rows, place], along[place, :])
            if turn > 0:
                tile = tile + raw[rows, :]
            if turn == 2:
                total = total + to_vreg(tile * tile)
            raw[rows, :] = tile
        return total

    totals = []

    def weights(turn):
        def one(which):
            if which == 0:
                total = weight_round(turn, 256, x_across, p_along, raw_in_ref)
            else:
                total = weight_round(turn, 128, a_across, g_along, raw_out_ref)
            if turn == 2:
                totals.append(total)

        return one

    bias[...] = jnp.zeros_like(bias)
    stages = {
        "h": lambda group: arrive(group, 0), "a": lambda group: arrive(group, 1),
        "0": forward, "1": pass_on, "3": activate, "4": spread,
        "6": backward, "7": hand_over, "x": keep_tokens, "b": keep_hidden,
        "v": weights(0), "w": weights(1), "u": weights(2),
    }
    forward(0)
    w_back_h[...], w_back_l[...] = split(w_in_f[...].T)
    for order in STEPS:
        for stage, which in zip(order[::2], order[1::2]):
            stages[stage](int(which))
    total = totals[0] + totals[1]

    def share(phase, place, value, peers):
        sums[phase, place] = value
        for peer in peers:
            slot = sums.at[phase, place]
            remote(slot, slot, s_send, s_recv.at[phase], *peer).start()

    def collect(phase):
        drain(sums.at[phase, pl.ds(0, 7)], s_recv.at[phase])
        return jnp.sum(sums[phase], axis=0)

    share(0, n, total, [(wide, lax.rem(n + j, NN)) for j in range(1, 8)])

    drain(gi_z, gz_recv)
    own_sum = gi[0, c]
    for j in range(FIRST_Y - 1):
        own_sum = own_sum + gi_z[j]
    gi[0, c] = own_sum
    for j in (2, 1, 3):
        to = lax.rem(y + j, NY)
        remote(gi.at[0, c, to], gi_y.at[j - 1], gy_send, gy_recv, at(z, to, c), n).start()
    total = collect(0)
    share(1, plane, total, [
        (z * NY * NC + lax.rem(plane + j, NY * NC), n) for j in range(1, 8)
    ])
    bias_in_ref[...] = jnp.sum(bias[...], axis=0, keepdims=True)
    bias_out_ref[...] = jnp.sum(xg[1].reshape(TOKENS, FEAT), axis=0, keepdims=True)
    to_owner(3)
    total = collect(1)
    share(2, z, total, [
        (lax.rem(z + j, NZ) * NY * NC + plane, n) for j in range(1, 8)
    ])
    to_owner(4)
    drain(gi_y, gy_recv)
    drain(gi_z_last, gzl_recv)
    grad_in_ref[...] = ((gi[0, c, y] + gi_y[0]) + (gi_y[1] + gi_y[2])) + (
        (gi_z_last[0] + gi_z_last[1]) + gi_z_last[2]
    )
    drain(xg.at[:, z, c, pl.ds(0, 3)], y_send)
    drain(xg.at[:, pl.ds(0, 7), 0], z_send)
    drain(xg.at[:, :, 0], c_send)
    drain(relay, f_send)
    drain(near, n_send)
    drain(ag.at[pl.ds(0, 7)], a_send)
    drain(gi_core, gc_send)
    drain(gi_z, gz_send)
    drain(gi_y, gy_send)
    drain(gi_y_first, gyf_send)
    drain(gi_z_last, gzl_send)
    total = jnp.sum(collect(2), keepdims=True)
    factor = jnp.minimum(1.0, math.sqrt(1.0 * D * FF * TOKENS) / (jnp.sqrt(total) + 1e-06))
    factor_ref[...] = jnp.broadcast_to(factor, factor_ref.shape)
    drain(sums.at[:, pl.ds(0, 7)], s_send)


PIECES = 3


def scale_kernel(
    grad_in_ref, raw_in_ref, raw_out_ref, bias_in_ref, bias_out_ref, factor_ref,
    grad_in_out, gw_in, gw_out, gb_in, gb_out, buf_in, buf_out, sems,
):
    factor = factor_ref[0:1, 0:1]
    stores = []
    for which, (raw, buf, out) in enumerate(
        ((raw_in_ref, buf_in, gw_in), (raw_out_ref, buf_out, gw_out))
    ):
        size = raw.shape[0] // PIECES
        for i in range(PIECES):
            rows = pl.ds(i * size, size)
            buf[rows, :] = raw[rows, :] * factor
            store = pltpu.make_async_copy(buf.at[rows], out.at[rows], sems.at[which, i])
            store.start()
            stores.append(store)
    grad_in_out[...] = grad_in_ref[...]
    gb_in[...] = (bias_in_ref[...] * factor)[0]
    gb_out[...] = (bias_out_ref[...] * factor)[0]
    for store in stores:
        store.wait()


def local(x_tokens, grad_out, w_in, b_in, w_out):
    vmem = pl.BlockSpec(memory_space=pltpu.VMEM)
    anywhere = pl.BlockSpec(memory_space=pl.ANY)
    dma = pltpu.SemaphoreType.DMA
    grad_in, raw_in, raw_out, bias_in, bias_out, factor = pl.pallas_call(
        kernel,
        out_shape=(
            jax.ShapeDtypeStruct((ROWS, FEAT), F32),
            jax.ShapeDtypeStruct((FEAT, HID), F32),
            jax.ShapeDtypeStruct((HID, FEAT), F32),
            jax.ShapeDtypeStruct((1, HID), F32),
            jax.ShapeDtypeStruct((1, FEAT), F32),
            jax.ShapeDtypeStruct((8, 128), F32),
        ),
        in_specs=[pl.BlockSpec(memory_space=pltpu.HBM)] * 5,
        out_specs=(vmem, vmem, vmem, vmem, vmem, vmem),
        scratch_shapes=[
            pltpu.VMEM((2, NZ, NC, NY, ROWS, FEAT), F32),
            pltpu.VMEM((NN, NZ, 2, ROWS, HID), F32),
            pltpu.VMEM((2, NZ, 2, ROWS, HID), F32),
            pltpu.VMEM((5, NZ, 2, ROWS, HID), F32),
            pltpu.VMEM((NN, NZ, 2, ROWS, HID), F32),
            pltpu.VMEM((NZ, NC, NY, ROWS, FEAT), F32),
            pltpu.VMEM((NZ, NY, ROWS, FEAT), F32),
            pltpu.VMEM((FIRST_Y - 1, NY, ROWS, FEAT), F32),
            pltpu.VMEM((NY - 1, ROWS, FEAT), F32),
            pltpu.VMEM((NY - 1, NZ - FIRST_Y, ROWS, FEAT), F32),
            pltpu.VMEM((NZ - FIRST_Y, ROWS, FEAT), F32),
            pltpu.VMEM((3, 8, 8, 128), F32),
            pltpu.VMEM((FEAT, HID), F32),
            pltpu.VMEM((HID, FEAT), F32),
            pltpu.VMEM((FEAT, HID), BF16),
            pltpu.VMEM((FEAT, HID), BF16),
            pltpu.VMEM((FEAT, HID), BF16),
            pltpu.VMEM((FEAT, HID), BF16),
            pltpu.VMEM((HID, FEAT), BF16),
            pltpu.VMEM((HID, FEAT), BF16),
            pltpu.VMEM((FEAT, SUM_COLUMNS), BF16),
            pltpu.VMEM((SUM_COLUMNS, FEAT), BF16),
            pltpu.VMEM((SUM_COLUMNS, HID), BF16),
            pltpu.VMEM((HID, SUM_COLUMNS), BF16),
            pltpu.VMEM((ROWS, HID), F32),
            pltpu.VMEM((HID,), F32),
            dma((5,)),
            dma, dma((NY - 1,)),
            dma, dma((NZ, 2)),
            dma, dma((NZ,)),
            dma, dma((5,)),
            dma, dma((5,)),
            dma, dma((5,)), dma((5,)),
            dma, dma((5,)),
            dma, dma,
            dma, dma,
            dma, dma((2,)),
            dma, dma,
            dma, dma((3,)),
        ],
        compiler_params=pltpu.CompilerParams(
            collective_id=0, has_side_effects=True, vmem_limit_bytes=51 * 1024 * 1024
        ),
    )(x_tokens, grad_out, w_in, b_in, w_out)
    return pl.pallas_call(
        scale_kernel,
        out_shape=(
            jax.ShapeDtypeStruct((ROWS, FEAT), F32),
            jax.ShapeDtypeStruct((FEAT, HID), F32),
            jax.ShapeDtypeStruct((HID, FEAT), F32),
            jax.ShapeDtypeStruct((HID,), F32),
            jax.ShapeDtypeStruct((FEAT,), F32),
        ),
        in_specs=[vmem, vmem, vmem, vmem, vmem, vmem],
        out_specs=(vmem, anywhere, anywhere, vmem, vmem),
        scratch_shapes=[
            pltpu.VMEM((FEAT, HID), F32),
            pltpu.VMEM((HID, FEAT), F32),
            dma((2, PIECES)),
        ],
        compiler_params=pltpu.CompilerParams(vmem_limit_bytes=16 * 1024 * 1024),
    )(grad_in, raw_in, raw_out, bias_in, bias_out, factor)


def solution(mesh):
    placed = (
        P("wide", "narrow"),
        P("wide", "narrow"),
        P("narrow", "wide"),
        P("wide"),
        P("wide", "narrow"),
    )
    return jax.shard_map(
        local,
        mesh=mesh,
        in_specs=placed,
        out_specs=(
            P("wide", "narrow"),
            P("narrow", "wide"),
            P("wide", "narrow"),
            P("wide"),
            P("narrow"),
        ),
        check_vma=False,
    )
```

```python
import math

import jax
import jax.numpy as jnp
from jax import lax
from jax.experimental import pallas as pl
from jax.experimental.pallas import tpu as pltpu
from jax.sharding import PartitionSpec as P

D = 6144
FF = 24576
TOKENS = 512
MESH = pl.DeviceIdType.MESH
F32, BF16 = jnp.float32, jnp.bfloat16

NZ, NY, NC, NN = 8, 4, 2, 8
ROWS = 8
BLOCK = NY * NC * ROWS
NX = 4
GROUPS = ((0, 1), (1, 2), (3, 2), (5, 2), (7, 1))
PLACES = ((1152, 128, 0), (0, 256, 0), (0, 256, 128), (768, 128, 0), (1152, 128, 64))
ROUNDS = ((0, 768), (768, 384), (1152, 384))
SUM_COLUMNS = 1536
FIRST_Y = 7
STEPS = (
    "x0h1a11001x1h230a211h30240x231a3h41203a460b0x3410470",
    "32x41361b1147142333462b2v043v1724463b3w073w164b4u0u1",
)
FEAT, HID = 768, 384

tanh_scale = math.sqrt(2.0 / math.pi)
cubic_weight = 0.044715


def gelu_parts(pre):
    inner = tanh_scale * (pre + cubic_weight * pre * pre * pre)
    tangent = jnp.tanh(inner)
    value = 0.5 * pre * (1.0 + tangent)
    slope = 0.5 * (1.0 + tangent) + 0.5 * pre * (1.0 - tangent * tangent) * tanh_scale * (
        1.0 + 3.0 * cubic_weight * pre * pre
    )
    return (value, slope)


def split(values):
    high = values.astype(BF16)
    return high, (values - high.astype(F32)).astype(BF16)


def product(left, right):
    return jnp.dot(left, right, preferred_element_type=F32)


def dot3(pair, high, low):
    rows = pair[0].shape[0]
    both = product(jnp.concatenate(pair, axis=0), high)
    return (both[:rows] + both[rows:]) + product(pair[0], low)


def remote(source, target, send, recv, wide, narrow):
    return pltpu.make_async_remote_copy(
        src_ref=source,
        dst_ref=target,
        send_sem=send,
        recv_sem=recv,
        device_id=(wide, narrow),
        device_id_type=MESH,
    )


def drain(ref, sem):
    pltpu.make_async_copy(ref, ref, sem).wait()


def kernel(
    x_ref, g_ref, w_in_ref, b_ref, w_out_ref,
    grad_in_ref, raw_in_ref, raw_out_ref, bias_in_ref, bias_out_ref, factor_ref,
    xg, part, relay, near, ag, gi, gi_core, gi_z, gi_y, gi_y_first, gi_z_last, sums,
    w_in_f, w_out_f, w_in_h, w_in_l, w_out_h, w_out_l, w_back_h, w_back_l,
    x_across, g_along, p_along, a_across, bias, b_here,
    load_sem, y_send, y_recv, z_send, z_recv, c_send, c_recv,
    f_send, f_recv, n_send, n_recv, a_send, a_one_recv, a_far_recv,
    gc_send, gc_recv, gz_send, gz_recv, gy_send, gy_recv, gyf_send, gyf_recv, gzl_send, gzl_recv,
    s_send, s_recv,
):
    wide = lax.axis_index("wide")
    n = lax.axis_index("narrow")
    z = lax.div(wide, NY * NC)
    y = lax.rem(lax.div(wide, NC), NY)
    c = lax.rem(wide, NC)

    yl = lax.div(n, NX)
    x = lax.rem(n, NX)
    right, left, far = (lax.rem(x + j, NX) for j in (1, 3, 2))
    over = (1 - yl) * NX + x

    def at(zz, yy, cc):
        return (zz * NY + yy) * NC + cc

    load_in = pltpu.make_async_copy(w_in_ref, w_in_f, load_sem.at[0])
    load_out = pltpu.make_async_copy(w_out_ref, w_out_f, load_sem.at[1])
    load_x = pltpu.make_async_copy(x_ref, xg.at[0, z, c, y], load_sem.at[2])
    load_g = pltpu.make_async_copy(g_ref, xg.at[1, z, c, y], load_sem.at[3])
    load_b = pltpu.make_async_copy(b_ref, b_here, load_sem.at[4])
    for load in (load_x, load_g, load_in, load_out, load_b):
        load.start()

    plane = lax.rem(wide, NY * NC)
    barrier = pltpu.get_barrier_semaphore()
    for j in range(1, 8):
        for peer in (
            (wide, lax.rem(n + j, NN)),
            (z * NY * NC + lax.rem(plane + j, NY * NC), n),
            (lax.rem(z + j, NZ) * NY * NC + plane, n),
        ):
            pl.semaphore_signal(barrier, inc=1, device_id=peer, device_id_type=MESH)
    load_x.wait()
    load_g.wait()
    pl.semaphore_wait(barrier, 21)

    def first_row(row):
        part_of = xg.at[:, z, c, row]
        for k in (1, 2):
            to = at(lax.rem(z + (NZ - 1 if k == 2 else 1), NZ), y, c)
            remote(part_of, part_of, z_send, z_recv.at[k, 0], to, n).start()
        remote(part_of, part_of, c_send, c_recv.at[0], at(z, y, 1 - c), n).start()

    def next_row(j):
        row = lax.rem(y + NY - j, NY)
        drain(xg.at[:, z, c, row], y_recv.at[j - 1])
        first_row(row)

    own = xg.at[:, z, c, y]
    for j in (1, 3, 2):
        remote(own, own, y_send, y_recv.at[j - 1], at(z, lax.rem(y + j, NY), c), n).start()
    first_row(y)
    load_in.wait()
    w_in_h[...], w_in_l[...] = split(w_in_f[...])
    next_row(1)
    next_row(3)
    load_out.wait()
    w_out_h[...], w_out_l[...] = split(w_out_f[...].T)
    load_b.wait()
    next_row(2)

    def block_of(k):
        return lax.rem(z + NZ + (1 - 2 * (k % 2)) * ((k + 1) // 2), NZ)

    def arrive(group, array):
        first, count = GROUPS[group]
        for k in range(first, first + count):
            here = xg.at[array, block_of(k), c]
            if group > 1:
                drain(here, z_recv.at[k, array])
            elif array == 0:
                drain(xg.at[:, block_of(k), c], z_recv.at[k, 0])
            if k < 5 or k - 5 == array:
                onward = at(lax.rem(z + NZ - 1 + 2 * (k % 2), NZ), y, c)
                remote(here, here, z_send, z_recv.at[k + 2 if k < 5 else 7, array], onward, n).start()
        for k in range(first, first + count):
            here = xg.at[array, block_of(k), c]
            remote(here, here, c_send, c_recv.at[k], at(z, y, 1 - c), n).start()

    def tokens(array, group):
        first, count = GROUPS[group]
        return jnp.concatenate(
            [xg[array, block_of(k)].reshape(BLOCK, FEAT) for k in range(first, first + count)], axis=0
        )

    def hidden(which, group):
        first, count = GROUPS[group]
        return jnp.concatenate(
            [ag[:, k, which].reshape(BLOCK, HID) for k in range(first, first + count)], axis=0
        )

    def forward(group):
        first, count = GROUPS[group]
        for k in range(first, first + count):
            drain(xg.at[:, block_of(k), 1 - c], c_recv.at[k])
        pre = dot3(split(tokens(0, group)), w_in_h[...], w_in_l[...])
        grad_act = dot3(split(tokens(1, group)), w_out_h[...], w_out_l[...])
        for b in range(count):
            rows = slice(b * BLOCK, (b + 1) * BLOCK)
            part[:, first + b, 0] = pre[rows].reshape(NN, ROWS, HID)
            part[:, first + b, 1] = grad_act[rows].reshape(NN, ROWS, HID)
        some = pl.ds(first, count)
        to_right, to_left = yl * NX + right, yl * NX + left
        remote(part.at[far, some], relay.at[0, some], f_send, f_recv.at[group], wide, to_right).start()
        remote(part.at[NX + far, some], relay.at[1, some], f_send, f_recv.at[group], wide, to_left).start()
        for owner, slot in ((NX + right, 3 - 2 * yl), (left, 2 + 2 * yl), (over, 0)):
            remote(part.at[owner, some], near.at[slot, some], n_send, n_recv.at[group], wide, owner).start()

    def keep_tokens(group):
        column, third, start = PLACES[group]
        size = GROUPS[group][1] * BLOCK
        across, along = split(tokens(0, group).T), split(tokens(1, group))
        for i in range(3):
            place = slice(column + third * i + start, column + third * i + start + size)
            x_across[:, place] = across[(0, 1, 0)[i]]
            g_along[place, :] = along[(0, 0, 1)[i]]

    def pass_on(group):
        some = pl.ds(*GROUPS[group])
        drain(relay.at[:, some], f_recv.at[group])
        part[right, some] += relay[0, some]
        part[NX + left, some] += relay[1, some]
        for owner, slot in ((right, 1 + 2 * yl), (NX + left, 4 - 2 * yl)):
            remote(part.at[owner, some], near.at[slot, some], n_send, n_recv.at[group], wide, owner).start()

    def activate(group):
        some = pl.ds(*GROUPS[group])
        drain(near.at[:, some], n_recv.at[group])
        total = part[n, some]
        for j in range(5):
            total = total + near[j, some]
        act, slope = gelu_parts(total[:, 0] + b_here[...])
        ag[n, some, 0] = act
        ag[n, some, 1] = total[:, 1] * slope
        mine = ag.at[n, some]
        for peer in (right, NX + right, left, NX + left, over):
            remote(mine, mine, a_send, a_one_recv.at[group], wide, peer).start()

    def spread(group):
        some = pl.ds(*GROUPS[group])
        drain(ag.at[pl.ds(0, 5), some], a_one_recv.at[group])
        for owner, peer in ((left, yl * NX + right), (NX + right, yl * NX + left)):
            chunk = ag.at[owner, some]
            remote(chunk, chunk, a_send, a_far_recv.at[group], wide, peer).start()

    def backward(group):
        first, count = GROUPS[group]
        some = pl.ds(first, count)
        drain(ag.at[pl.ds(0, 2), some], a_far_recv.at[group])
        grad = dot3(split(hidden(1, group)), w_back_h[...], w_back_l[...])
        gi[some] = grad.reshape(count, NC, NY, ROWS, FEAT)
        remote(
            gi.at[some, 1 - c], gi_core.at[some], gc_send, gc_recv.at[group], at(z, y, 1 - c), n
        ).start()

    def keep_hidden(group):
        column, third, start = PLACES[group]
        size = GROUPS[group][1] * BLOCK
        grad_pre = hidden(1, group)
        bias[...] += jnp.sum(grad_pre.reshape(size // 8, 8, HID), axis=0)
        across, along = split(hidden(0, group).T), split(grad_pre)
        for i in range(3):
            place = slice(column + third * i + start, column + third * i + start + size)
            a_across[:, place] = across[(0, 1, 0)[i]]
            p_along[place, :] = along[(0, 0, 1)[i]]

    def hand_over(group):
        first, count = GROUPS[group]
        drain(gi_core.at[pl.ds(first, count)], gc_recv.at[group])
        for k in range(first, first + count):
            gi[k, c] += gi_core[k]
            if 0 < k < FIRST_Y:
                remote(
                    gi.at[k, c], gi_z.at[k - 1], gz_send, gz_recv, at(block_of(k), y, c), n
                ).start()
        if first >= FIRST_Y:
            for j in (2, 1, 3):
                to = lax.rem(y + j, NY)
                remote(
                    gi.at[pl.ds(first, count), c, to],
                    gi_y_first.at[j - 1, pl.ds(first - FIRST_Y, count)],
                    gyf_send, gyf_recv, at(z, to, c), n,
                ).start()

    def to_owner(group):
        first, count = GROUPS[group]
        drain(gi_y_first, gyf_recv)
        for k in range(first, first + count):
            i = k - FIRST_Y
            gi[k, c, y] += gi_y_first[0, i] + (gi_y_first[1, i] + gi_y_first[2, i])
            remote(
                gi.at[k, c, y], gi_z_last.at[i], gzl_send, gzl_recv, at(block_of(k), y, c), n
            ).start()

    def to_vreg(squares):
        rows, columns = squares.shape
        lanes = jnp.sum(squares.reshape(rows // 8, 8, columns), axis=0)
        out = lanes[:, :128]
        for j in range(1, columns // 128):
            out = out + lanes[:, 128 * j:128 * (j + 1)]
        return out

    def weight_round(turn, size, across, along, raw):
        place = slice(ROUNDS[turn][0], sum(ROUNDS[turn]))
        total = jnp.zeros((8, 128), F32)
        for start in range(0, raw.shape[0], size):
            rows = slice(start, start + size)
            tile = product(across[rows, place], along[place, :])
            if turn > 0:
                tile = tile + raw[rows, :]
            if turn == 2:
                total = total + to_vreg(tile * tile)
            raw[rows, :] = tile
        return total

    totals = []

    def weights(turn):
        def one(which):
            if which == 0:
                total = weight_round(turn, 256, x_across, p_along, raw_in_ref)
            else:
                total = weight_round(turn, 128, a_across, g_along, raw_out_ref)
            if turn == 2:
                totals.append(total)

        return one

    bias[...] = jnp.zeros_like(bias)
    stages = {
        "h": lambda group: arrive(group, 0), "a": lambda group: arrive(group, 1),
        "0": forward, "1": pass_on, "3": activate, "4": spread,
        "6": backward, "7": hand_over, "x": keep_tokens, "b": keep_hidden,
        "v": weights(0), "w": weights(1), "u": weights(2),
    }
    forward(0)
    w_back_h[...], w_back_l[...] = split(w_in_f[...].T)
    for order in STEPS:
        for stage, which in zip(order[::2], order[1::2]):
            stages[stage](int(which))
    total = totals[0] + totals[1]

    def share(phase, place, value, peers):
        sums[phase, place] = value
        for peer in peers:
            slot = sums.at[phase, place]
            remote(slot, slot, s_send, s_recv.at[phase], *peer).start()

    def collect(phase):
        drain(sums.at[phase, pl.ds(0, 7)], s_recv.at[phase])
        return jnp.sum(sums[phase], axis=0)

    share(0, n, total, [(wide, lax.rem(n + j, NN)) for j in range(1, 8)])

    hand_over(4)
    total = collect(0)
    share(1, plane, total, [
        (z * NY * NC + lax.rem(plane + j, NY * NC), n) for j in range(1, 8)
    ])
    to_owner(4)
    drain(gi_z, gz_recv)
    own_sum = gi[0, c]
    for j in range(FIRST_Y - 1):
        own_sum = own_sum + gi_z[j]
    gi[0, c] = own_sum
    for j in (2, 1, 3):
        to = lax.rem(y + j, NY)
        remote(gi.at[0, c, to], gi_y.at[j - 1], gy_send, gy_recv, at(z, to, c), n).start()
    bias_in_ref[...] = jnp.sum(bias[...], axis=0, keepdims=True)
    bias_out_ref[...] = jnp.sum(xg[1].reshape(TOKENS, FEAT), axis=0, keepdims=True)
    total = collect(1)
    share(2, z, total, [
        (lax.rem(z + j, NZ) * NY * NC + plane, n) for j in range(1, 8)
    ])
    drain(gi_y, gy_recv)
    drain(gi_z_last, gzl_recv)
    grad_in_ref[...] = ((gi[0, c, y] + gi_y[0]) + (gi_y[1] + gi_y[2])) + gi_z_last[0]
    drain(xg.at[:, z, c, pl.ds(0, 3)], y_send)
    drain(xg.at[:, pl.ds(0, 7), 0], z_send)
    drain(xg.at[:, :, 0], c_send)
    drain(relay, f_send)
    drain(near, n_send)
    drain(ag.at[pl.ds(0, 7)], a_send)
    drain(gi_core, gc_send)
    drain(gi_z, gz_send)
    drain(gi_y, gy_send)
    drain(gi_y_first, gyf_send)
    drain(gi_z_last, gzl_send)
    total = jnp.sum(collect(2), keepdims=True)
    factor = jnp.minimum(1.0, math.sqrt(1.0 * D * FF * TOKENS) / (jnp.sqrt(total) + 1e-06))
    factor_ref[...] = jnp.broadcast_to(factor, factor_ref.shape)
    drain(sums.at[:, pl.ds(0, 7)], s_send)


PIECES = 3


def scale_kernel(
    grad_in_ref, raw_in_ref, raw_out_ref, bias_in_ref, bias_out_ref, factor_ref,
    grad_in_out, gw_in, gw_out, gb_in, gb_out, buf_in, buf_out, sems,
):
    factor = factor_ref[0:1, 0:1]
    stores = []
    for which, (raw, buf, out) in enumerate(
        ((raw_in_ref, buf_in, gw_in), (raw_out_ref, buf_out, gw_out))
    ):
        size = raw.shape[0] // PIECES
        for i in range(PIECES):
            rows = pl.ds(i * size, size)
            buf[rows, :] = raw[rows, :] * factor
            store = pltpu.make_async_copy(buf.at[rows], out.at[rows], sems.at[which, i])
            store.start()
            stores.append(store)
    grad_in_out[...] = grad_in_ref[...]
    gb_in[...] = (bias_in_ref[...] * factor)[0]
    gb_out[...] = (bias_out_ref[...] * factor)[0]
    for store in stores:
        store.wait()


def local(x_tokens, grad_out, w_in, b_in, w_out):
    vmem = pl.BlockSpec(memory_space=pltpu.VMEM)
    anywhere = pl.BlockSpec(memory_space=pl.ANY)
    dma = pltpu.SemaphoreType.DMA
    grad_in, raw_in, raw_out, bias_in, bias_out, factor = pl.pallas_call(
        kernel,
        out_shape=(
            jax.ShapeDtypeStruct((ROWS, FEAT), F32),
            jax.ShapeDtypeStruct((FEAT, HID), F32),
            jax.ShapeDtypeStruct((HID, FEAT), F32),
            jax.ShapeDtypeStruct((1, HID), F32),
            jax.ShapeDtypeStruct((1, FEAT), F32),
            jax.ShapeDtypeStruct((8, 128), F32),
        ),
        in_specs=[pl.BlockSpec(memory_space=pltpu.HBM)] * 5,
        out_specs=(vmem, vmem, vmem, vmem, vmem, vmem),
        scratch_shapes=[
            pltpu.VMEM((2, NZ, NC, NY, ROWS, FEAT), F32),
            pltpu.VMEM((NN, NZ, 2, ROWS, HID), F32),
            pltpu.VMEM((2, NZ, 2, ROWS, HID), F32),
            pltpu.VMEM((5, NZ, 2, ROWS, HID), F32),
            pltpu.VMEM((NN, NZ, 2, ROWS, HID), F32),
            pltpu.VMEM((NZ, NC, NY, ROWS, FEAT), F32),
            pltpu.VMEM((NZ, NY, ROWS, FEAT), F32),
            pltpu.VMEM((FIRST_Y - 1, NY, ROWS, FEAT), F32),
            pltpu.VMEM((NY - 1, ROWS, FEAT), F32),
            pltpu.VMEM((NY - 1, NZ - FIRST_Y, ROWS, FEAT), F32),
            pltpu.VMEM((NZ - FIRST_Y, ROWS, FEAT), F32),
            pltpu.VMEM((3, 8, 8, 128), F32),
            pltpu.VMEM((FEAT, HID), F32),
            pltpu.VMEM((HID, FEAT), F32),
            pltpu.VMEM((FEAT, HID), BF16),
            pltpu.VMEM((FEAT, HID), BF16),
            pltpu.VMEM((FEAT, HID), BF16),
            pltpu.VMEM((FEAT, HID), BF16),
            pltpu.VMEM((HID, FEAT), BF16),
            pltpu.VMEM((HID, FEAT), BF16),
            pltpu.VMEM((FEAT, SUM_COLUMNS), BF16),
            pltpu.VMEM((SUM_COLUMNS, FEAT), BF16),
            pltpu.VMEM((SUM_COLUMNS, HID), BF16),
            pltpu.VMEM((HID, SUM_COLUMNS), BF16),
            pltpu.VMEM((ROWS, HID), F32),
            pltpu.VMEM((HID,), F32),
            dma((5,)),
            dma, dma((NY - 1,)),
            dma, dma((NZ, 2)),
            dma, dma((NZ,)),
            dma, dma((5,)),
            dma, dma((5,)),
            dma, dma((5,)), dma((5,)),
            dma, dma((5,)),
            dma, dma,
            dma, dma,
            dma, dma,
            dma, dma,
            dma, dma((3,)),
        ],
        compiler_params=pltpu.CompilerParams(
            collective_id=0, has_side_effects=True, vmem_limit_bytes=51 * 1024 * 1024
        ),
    )(*(pltpu.with_memory_space_constraint(a, pltpu.HBM) for a in (x_tokens, grad_out, w_in, b_in, w_out)))
    return pl.pallas_call(
        scale_kernel,
        out_shape=(
            jax.ShapeDtypeStruct((ROWS, FEAT), F32),
            jax.ShapeDtypeStruct((FEAT, HID), F32),
            jax.ShapeDtypeStruct((HID, FEAT), F32),
            jax.ShapeDtypeStruct((HID,), F32),
            jax.ShapeDtypeStruct((FEAT,), F32),
        ),
        in_specs=[vmem, vmem, vmem, vmem, vmem, vmem],
        out_specs=(vmem, anywhere, anywhere, vmem, vmem),
        scratch_shapes=[
            pltpu.VMEM((FEAT, HID), F32),
            pltpu.VMEM((HID, FEAT), F32),
            dma((2, PIECES)),
        ],
        compiler_params=pltpu.CompilerParams(vmem_limit_bytes=16 * 1024 * 1024),
    )(grad_in, raw_in, raw_out, bias_in, bias_out, factor)


def solution(mesh):
    placed = (
        P("wide", "narrow"),
        P("wide", "narrow"),
        P("narrow", "wide"),
        P("wide"),
        P("wide", "narrow"),
    )
    return jax.shard_map(
        local,
        mesh=mesh,
        in_specs=placed,
        out_specs=(
            P("wide", "narrow"),
            P("narrow", "wide"),
            P("wide", "narrow"),
            P("wide"),
            P("narrow"),
        ),
        check_vma=False,
    )
```

```python
import math

import jax
import jax.numpy as jnp
from jax import lax
from jax.experimental import pallas as pl
from jax.experimental.pallas import tpu as pltpu
from jax.sharding import PartitionSpec as P

D = 6144
FF = 24576
TOKENS = 512
MESH = pl.DeviceIdType.MESH
F32, BF16 = jnp.float32, jnp.bfloat16

NZ, NY, NC, NN = 8, 4, 2, 8
ROWS = 8
BLOCK = NY * NC * ROWS
NX = 4
GROUPS = ((0, 1), (1, 2), (3, 2), (5, 2), (7, 1))
PLACES = ((1152, 128, 0), (0, 256, 0), (0, 256, 128), (768, 128, 0), (1152, 128, 64))
ROUNDS = ((0, 768), (768, 384), (1152, 384))
SUM_COLUMNS = 1536
FIRST_Y = 7
STEPS = (
    "x0h1a11001x1h230a211h30240x231a3h41203a460x3b0410470",
    "x4133261b114337142346243b2v0v1724463b3w0w16473b4u0u1",
)
FEAT, HID = 768, 384

tanh_scale = math.sqrt(2.0 / math.pi)
cubic_weight = 0.044715


def gelu_parts(pre):
    inner = tanh_scale * (pre + cubic_weight * pre * pre * pre)
    tangent = jnp.tanh(inner)
    value = 0.5 * pre * (1.0 + tangent)
    slope = 0.5 * (1.0 + tangent) + 0.5 * pre * (1.0 - tangent * tangent) * tanh_scale * (
        1.0 + 3.0 * cubic_weight * pre * pre
    )
    return (value, slope)


def split(values):
    high = values.astype(BF16)
    return high, (values - high.astype(F32)).astype(BF16)


def product(left, right):
    return jnp.dot(left, right, preferred_element_type=F32)


def dot3(pair, high, low):
    rows = pair[0].shape[0]
    both = product(jnp.concatenate(pair, axis=0), high)
    return (both[:rows] + both[rows:]) + product(pair[0], low)


def remote(source, target, send, recv, wide, narrow):
    return pltpu.make_async_remote_copy(
        src_ref=source,
        dst_ref=target,
        send_sem=send,
        recv_sem=recv,
        device_id=(wide, narrow),
        device_id_type=MESH,
    )


def drain(ref, sem):
    pltpu.make_async_copy(ref, ref, sem).wait()


def kernel(
    x_ref, g_ref, w_in_ref, b_ref, w_out_ref,
    grad_in_ref, raw_in_ref, raw_out_ref, bias_in_ref, bias_out_ref, factor_ref,
    xg, part, relay, near, ag, gi, gi_core, gi_z, gi_y, gi_y_first, gi_z_last, sums,
    w_in_f, w_out_f, w_in_h, w_in_l, w_out_h, w_out_l, w_back_h, w_back_l,
    x_across, g_along, p_along, a_across, bias, b_here,
    load_sem, y_send, y_recv, z_send, z_recv, c_send, c_recv,
    f_send, f_recv, n_send, n_recv, a_send, a_one_recv, a_far_recv,
    gc_send, gc_recv, gz_send, gz_recv, gy_send, gy_recv, gyf_send, gyf_recv, gzl_send, gzl_recv,
    s_send, s_recv,
):
    wide = lax.axis_index("wide")
    n = lax.axis_index("narrow")
    z = lax.div(wide, NY * NC)
    y = lax.rem(lax.div(wide, NC), NY)
    c = lax.rem(wide, NC)

    yl = lax.div(n, NX)
    x = lax.rem(n, NX)
    right, left, far = (lax.rem(x + j, NX) for j in (1, 3, 2))
    over = (1 - yl) * NX + x

    def at(zz, yy, cc):
        return (zz * NY + yy) * NC + cc

    load_in = pltpu.make_async_copy(w_in_ref, w_in_f, load_sem.at[0])
    load_out = pltpu.make_async_copy(w_out_ref, w_out_f, load_sem.at[1])
    load_x = pltpu.make_async_copy(x_ref, xg.at[0, z, c, y], load_sem.at[2])
    load_g = pltpu.make_async_copy(g_ref, xg.at[1, z, c, y], load_sem.at[3])
    load_b = pltpu.make_async_copy(b_ref, b_here, load_sem.at[4])
    for load in (load_x, load_g, load_in, load_out, load_b):
        load.start()

    plane = lax.rem(wide, NY * NC)
    barrier = pltpu.get_barrier_semaphore()
    for j in range(1, 8):
        for peer in (
            (wide, lax.rem(n + j, NN)),
            (z * NY * NC + lax.rem(plane + j, NY * NC), n),
            (lax.rem(z + j, NZ) * NY * NC + plane, n),
        ):
            pl.semaphore_signal(barrier, inc=1, device_id=peer, device_id_type=MESH)
    load_x.wait()
    load_g.wait()
    pl.semaphore_wait(barrier, 21)

    def first_row(row):
        part_of = xg.at[:, z, c, row]
        for k in (1, 2):
            to = at(lax.rem(z + (NZ - 1 if k == 2 else 1), NZ), y, c)
            remote(part_of, part_of, z_send, z_recv.at[k, 0], to, n).start()
        remote(part_of, part_of, c_send, c_recv.at[0], at(z, y, 1 - c), n).start()

    def next_row(j):
        row = lax.rem(y + NY - j, NY)
        drain(xg.at[:, z, c, row], y_recv.at[j - 1])
        first_row(row)

    own = xg.at[:, z, c, y]
    for j in (1, 3, 2):
        remote(own, own, y_send, y_recv.at[j - 1], at(z, lax.rem(y + j, NY), c), n).start()
    first_row(y)
    load_in.wait()
    w_in_h[...], w_in_l[...] = split(w_in_f[...])
    next_row(1)
    next_row(3)
    load_out.wait()
    w_out_h[...], w_out_l[...] = split(w_out_f[...].T)
    load_b.wait()
    next_row(2)

    def block_of(k):
        return lax.rem(z + NZ + (1 - 2 * (k % 2)) * ((k + 1) // 2), NZ)

    def arrive(group, array):
        first, count = GROUPS[group]
        for k in range(first, first + count):
            here = xg.at[array, block_of(k), c]
            if group > 1:
                drain(here, z_recv.at[k, array])
            elif array == 0:
                drain(xg.at[:, block_of(k), c], z_recv.at[k, 0])
            if k < 5 or k - 5 == array:
                onward = at(lax.rem(z + NZ - 1 + 2 * (k % 2), NZ), y, c)
                remote(here, here, z_send, z_recv.at[k + 2 if k < 5 else 7, array], onward, n).start()
        for k in range(first, first + count):
            here = xg.at[array, block_of(k), c]
            remote(here, here, c_send, c_recv.at[k], at(z, y, 1 - c), n).start()

    def tokens(array, group):
        first, count = GROUPS[group]
        return jnp.concatenate(
            [xg[array, block_of(k)].reshape(BLOCK, FEAT) for k in range(first, first + count)], axis=0
        )

    def hidden(which, group):
        first, count = GROUPS[group]
        return jnp.concatenate(
            [ag[:, k, which].reshape(BLOCK, HID) for k in range(first, first + count)], axis=0
        )

    def forward(group):
        first, count = GROUPS[group]
        for k in range(first, first + count):
            drain(xg.at[:, block_of(k), 1 - c], c_recv.at[k])
        pre = dot3(split(tokens(0, group)), w_in_h[...], w_in_l[...])
        grad_act = dot3(split(tokens(1, group)), w_out_h[...], w_out_l[...])
        for b in range(count):
            rows = slice(b * BLOCK, (b + 1) * BLOCK)
            part[:, first + b, 0] = pre[rows].reshape(NN, ROWS, HID)
            part[:, first + b, 1] = grad_act[rows].reshape(NN, ROWS, HID)
        some = pl.ds(first, count)
        to_right, to_left = yl * NX + right, yl * NX + left
        remote(part.at[far, some], relay.at[0, some], f_send, f_recv.at[group], wide, to_right).start()
        remote(part.at[NX + far, some], relay.at[1, some], f_send, f_recv.at[group], wide, to_left).start()
        for owner, slot in ((NX + right, 3 - 2 * yl), (left, 2 + 2 * yl), (over, 0)):
            remote(part.at[owner, some], near.at[slot, some], n_send, n_recv.at[group], wide, owner).start()

    def keep_tokens(group):
        column, third, start = PLACES[group]
        size = GROUPS[group][1] * BLOCK
        across, along = split(tokens(0, group).T), split(tokens(1, group))
        for i in range(3):
            place = slice(column + third * i + start, column + third * i + start + size)
            x_across[:, place] = across[(0, 1, 0)[i]]
            g_along[place, :] = along[(0, 0, 1)[i]]

    def pass_on(group):
        some = pl.ds(*GROUPS[group])
        drain(relay.at[:, some], f_recv.at[group])
        part[right, some] += relay[0, some]
        part[NX + left, some] += relay[1, some]
        for owner, slot in ((right, 1 + 2 * yl), (NX + left, 4 - 2 * yl)):
            remote(part.at[owner, some], near.at[slot, some], n_send, n_recv.at[group], wide, owner).start()

    def activate(group):
        some = pl.ds(*GROUPS[group])
        drain(near.at[:, some], n_recv.at[group])
        total = part[n, some]
        for j in range(5):
            total = total + near[j, some]
        act, slope = gelu_parts(total[:, 0] + b_here[...])
        ag[n, some, 0] = act
        ag[n, some, 1] = total[:, 1] * slope
        mine = ag.at[n, some]
        for peer in (right, NX + right, left, NX + left, over):
            remote(mine, mine, a_send, a_one_recv.at[group], wide, peer).start()

    def spread(group):
        some = pl.ds(*GROUPS[group])
        drain(ag.at[pl.ds(0, 5), some], a_one_recv.at[group])
        for owner, peer in ((left, yl * NX + right), (NX + right, yl * NX + left)):
            chunk = ag.at[owner, some]
            remote(chunk, chunk, a_send, a_far_recv.at[group], wide, peer).start()

    def backward(group):
        first, count = GROUPS[group]
        some = pl.ds(first, count)
        drain(ag.at[pl.ds(0, 2), some], a_far_recv.at[group])
        grad = dot3(split(hidden(1, group)), w_back_h[...], w_back_l[...])
        gi[some] = grad.reshape(count, NC, NY, ROWS, FEAT)
        remote(
            gi.at[some, 1 - c], gi_core.at[some], gc_send, gc_recv.at[group], at(z, y, 1 - c), n
        ).start()

    def keep_hidden(group):
        column, third, start = PLACES[group]
        size = GROUPS[group][1] * BLOCK
        grad_pre = hidden(1, group)
        bias[...] += jnp.sum(grad_pre.reshape(size // 8, 8, HID), axis=0)
        across, along = split(hidden(0, group).T), split(grad_pre)
        for i in range(3):
            place = slice(column + third * i + start, column + third * i + start + size)
            a_across[:, place] = across[(0, 1, 0)[i]]
            p_along[place, :] = along[(0, 0, 1)[i]]

    def hand_over(group):
        first, count = GROUPS[group]
        drain(gi_core.at[pl.ds(first, count)], gc_recv.at[group])
        for k in range(first, first + count):
            gi[k, c] += gi_core[k]
            if 0 < k < FIRST_Y:
                remote(
                    gi.at[k, c], gi_z.at[k - 1], gz_send, gz_recv, at(block_of(k), y, c), n
                ).start()
        if first >= FIRST_Y:
            for j in (2, 1, 3):
                to = lax.rem(y + j, NY)
                remote(
                    gi.at[pl.ds(first, count), c, to],
                    gi_y_first.at[j - 1, pl.ds(first - FIRST_Y, count)],
                    gyf_send, gyf_recv, at(z, to, c), n,
                ).start()

    def to_owner(group):
        first, count = GROUPS[group]
        drain(gi_y_first, gyf_recv)
        for k in range(first, first + count):
            i = k - FIRST_Y
            gi[k, c, y] += gi_y_first[0, i] + (gi_y_first[1, i] + gi_y_first[2, i])
            remote(
                gi.at[k, c, y], gi_z_last.at[i], gzl_send, gzl_recv, at(block_of(k), y, c), n
            ).start()

    def to_vreg(squares):
        rows, columns = squares.shape
        lanes = jnp.sum(squares.reshape(rows // 8, 8, columns), axis=0)
        out = lanes[:, :128]
        for j in range(1, columns // 128):
            out = out + lanes[:, 128 * j:128 * (j + 1)]
        return out

    def weight_round(turn, size, across, along, raw):
        place = slice(ROUNDS[turn][0], sum(ROUNDS[turn]))
        total = jnp.zeros((8, 128), F32)
        for start in range(0, raw.shape[0], size):
            rows = slice(start, start + size)
            tile = product(across[rows, place], along[place, :])
            if turn > 0:
                tile = tile + raw[rows, :]
            if turn == 2:
                total = total + to_vreg(tile * tile)
            raw[rows, :] = tile
        return total

    totals = []

    def weights(turn):
        def one(which):
            if which == 0:
                total = weight_round(turn, 256, x_across, p_along, raw_in_ref)
            else:
                total = weight_round(turn, 128, a_across, g_along, raw_out_ref)
            if turn == 2:
                totals.append(total)

        return one

    bias[...] = jnp.zeros_like(bias)
    stages = {
        "h": lambda group: arrive(group, 0), "a": lambda group: arrive(group, 1),
        "0": forward, "1": pass_on, "3": activate, "4": spread,
        "6": backward, "7": hand_over, "x": keep_tokens, "b": keep_hidden,
        "v": weights(0), "w": weights(1), "u": weights(2),
    }
    w_back_h[...], w_back_l[...] = split(w_in_f[...].T)
    forward(0)
    for order in STEPS:
        for stage, which in zip(order[::2], order[1::2]):
            stages[stage](int(which))
    total = totals[0] + totals[1]

    def share(phase, place, value, peers):
        sums[phase, place] = value
        for peer in peers:
            slot = sums.at[phase, place]
            remote(slot, slot, s_send, s_recv.at[phase], *peer).start()

    def collect(phase):
        drain(sums.at[phase, pl.ds(0, 7)], s_recv.at[phase])
        return jnp.sum(sums[phase], axis=0)

    share(0, n, total, [(wide, lax.rem(n + j, NN)) for j in range(1, 8)])

    hand_over(4)
    total = collect(0)
    share(1, plane, total, [
        (z * NY * NC + lax.rem(plane + j, NY * NC), n) for j in range(1, 8)
    ])
    to_owner(4)
    drain(gi_z, gz_recv)
    own_sum = gi[0, c]
    for j in range(FIRST_Y - 1):
        own_sum = own_sum + gi_z[j]
    gi[0, c] = own_sum
    for j in (2, 1, 3):
        to = lax.rem(y + j, NY)
        remote(gi.at[0, c, to], gi_y.at[j - 1], gy_send, gy_recv, at(z, to, c), n).start()
    bias_in_ref[...] = jnp.sum(bias[...], axis=0, keepdims=True)
    bias_out_ref[...] = jnp.sum(xg[1].reshape(TOKENS, FEAT), axis=0, keepdims=True)
    total = collect(1)
    share(2, z, total, [
        (lax.rem(z + j, NZ) * NY * NC + plane, n) for j in range(1, 8)
    ])
    drain(gi_y, gy_recv)
    drain(gi_z_last, gzl_recv)
    grad_in_ref[...] = ((gi[0, c, y] + gi_y[0]) + (gi_y[1] + gi_y[2])) + gi_z_last[0]
    drain(xg.at[:, z, c, pl.ds(0, 3)], y_send)
    drain(xg.at[:, pl.ds(0, 7), 0], z_send)
    drain(xg.at[:, :, 0], c_send)
    drain(relay, f_send)
    drain(near, n_send)
    drain(ag.at[pl.ds(0, 7)], a_send)
    drain(gi_core, gc_send)
    drain(gi_z, gz_send)
    drain(gi_y, gy_send)
    drain(gi_y_first, gyf_send)
    drain(gi_z_last, gzl_send)
    total = jnp.sum(collect(2), keepdims=True)
    factor = jnp.minimum(1.0, math.sqrt(1.0 * D * FF * TOKENS) / (jnp.sqrt(total) + 1e-06))
    factor_ref[...] = jnp.broadcast_to(factor, factor_ref.shape)
    drain(sums.at[:, pl.ds(0, 7)], s_send)


PIECES = 3


def scale_kernel(
    grad_in_ref, raw_in_ref, raw_out_ref, bias_in_ref, bias_out_ref, factor_ref,
    grad_in_out, gw_in, gw_out, gb_in, gb_out, buf_in, buf_out, bias_in, bias_out, sems, small_sems,
):
    factor = factor_ref[0:1, 0:1]
    bias_in[...] = (bias_in_ref[...] * factor)[0]
    bias_out[...] = (bias_out_ref[...] * factor)[0]
    stores = []
    for i, (source, out) in enumerate(
        ((grad_in_ref, grad_in_out), (bias_in, gb_in), (bias_out, gb_out))
    ):
        store = pltpu.make_async_copy(source, out, small_sems.at[i])
        store.start()
        stores.append(store)
    for which, (raw, buf, out) in enumerate(
        ((raw_in_ref, buf_in, gw_in), (raw_out_ref, buf_out, gw_out))
    ):
        size = raw.shape[0] // PIECES
        for i in range(PIECES):
            rows = pl.ds(i * size, size)
            buf[rows, :] = raw[rows, :] * factor
            store = pltpu.make_async_copy(buf.at[rows], out.at[rows], sems.at[which, i])
            store.start()
            stores.append(store)
    for store in stores:
        store.wait()


def local(x_tokens, grad_out, w_in, b_in, w_out):
    vmem = pl.BlockSpec(memory_space=pltpu.VMEM)
    anywhere = pl.BlockSpec(memory_space=pl.ANY)
    dma = pltpu.SemaphoreType.DMA
    grad_in, raw_in, raw_out, bias_in, bias_out, factor = pl.pallas_call(
        kernel,
        out_shape=(
            jax.ShapeDtypeStruct((ROWS, FEAT), F32),
            jax.ShapeDtypeStruct((FEAT, HID), F32),
            jax.ShapeDtypeStruct((HID, FEAT), F32),
            jax.ShapeDtypeStruct((1, HID), F32),
            jax.ShapeDtypeStruct((1, FEAT), F32),
            jax.ShapeDtypeStruct((8, 128), F32),
        ),
        in_specs=[pl.BlockSpec(memory_space=pltpu.HBM)] * 5,
        out_specs=(vmem, vmem, vmem, vmem, vmem, vmem),
        scratch_shapes=[
            pltpu.VMEM((2, NZ, NC, NY, ROWS, FEAT), F32),
            pltpu.VMEM((NN, NZ, 2, ROWS, HID), F32),
            pltpu.VMEM((2, NZ, 2, ROWS, HID), F32),
            pltpu.VMEM((5, NZ, 2, ROWS, HID), F32),
            pltpu.VMEM((NN, NZ, 2, ROWS, HID), F32),
            pltpu.VMEM((NZ, NC, NY, ROWS, FEAT), F32),
            pltpu.VMEM((NZ, NY, ROWS, FEAT), F32),
            pltpu.VMEM((FIRST_Y - 1, NY, ROWS, FEAT), F32),
            pltpu.VMEM((NY - 1, ROWS, FEAT), F32),
            pltpu.VMEM((NY - 1, NZ - FIRST_Y, ROWS, FEAT), F32),
            pltpu.VMEM((NZ - FIRST_Y, ROWS, FEAT), F32),
            pltpu.VMEM((3, 8, 8, 128), F32),
            pltpu.VMEM((FEAT, HID), F32),
            pltpu.VMEM((HID, FEAT), F32),
            pltpu.VMEM((FEAT, HID), BF16),
            pltpu.VMEM((FEAT, HID), BF16),
            pltpu.VMEM((FEAT, HID), BF16),
            pltpu.VMEM((FEAT, HID), BF16),
            pltpu.VMEM((HID, FEAT), BF16),
            pltpu.VMEM((HID, FEAT), BF16),
            pltpu.VMEM((FEAT, SUM_COLUMNS), BF16),
            pltpu.VMEM((SUM_COLUMNS, FEAT), BF16),
            pltpu.VMEM((SUM_COLUMNS, HID), BF16),
            pltpu.VMEM((HID, SUM_COLUMNS), BF16),
            pltpu.VMEM((ROWS, HID), F32),
            pltpu.VMEM((HID,), F32),
            dma((5,)),
            dma, dma((NY - 1,)),
            dma, dma((NZ, 2)),
            dma, dma((NZ,)),
            dma, dma((5,)),
            dma, dma((5,)),
            dma, dma((5,)), dma((5,)),
            dma, dma((5,)),
            dma, dma,
            dma, dma,
            dma, dma,
            dma, dma,
            dma, dma((3,)),
        ],
        compiler_params=pltpu.CompilerParams(
            collective_id=0, has_side_effects=True, vmem_limit_bytes=51 * 1024 * 1024
        ),
    )(*(pltpu.with_memory_space_constraint(a, pltpu.HBM) for a in (x_tokens, grad_out, w_in, b_in, w_out)))
    return pl.pallas_call(
        scale_kernel,
        out_shape=(
            jax.ShapeDtypeStruct((ROWS, FEAT), F32),
            jax.ShapeDtypeStruct((FEAT, HID), F32),
            jax.ShapeDtypeStruct((HID, FEAT), F32),
            jax.ShapeDtypeStruct((HID,), F32),
            jax.ShapeDtypeStruct((FEAT,), F32),
        ),
        in_specs=[vmem, vmem, vmem, vmem, vmem, vmem],
        out_specs=(anywhere,) * 5,
        scratch_shapes=[
            pltpu.VMEM((FEAT, HID), F32),
            pltpu.VMEM((HID, FEAT), F32),
            pltpu.VMEM((HID,), F32),
            pltpu.VMEM((FEAT,), F32),
            dma((2, PIECES)),
            dma((3,)),
        ],
        compiler_params=pltpu.CompilerParams(vmem_limit_bytes=16 * 1024 * 1024),
    )(grad_in, raw_in, raw_out, bias_in, bias_out, factor)


def solution(mesh):
    placed = (
        P("wide", "narrow"),
        P("wide", "narrow"),
        P("narrow", "wide"),
        P("wide"),
        P("wide", "narrow"),
    )
    return jax.shard_map(
        local,
        mesh=mesh,
        in_specs=placed,
        out_specs=(
            P("wide", "narrow"),
            P("narrow", "wide"),
            P("wide", "narrow"),
            P("wide"),
            P("narrow"),
        ),
        check_vma=False,
    )
```

```python
import math

import jax
import jax.numpy as jnp
from jax import lax
from jax.experimental import pallas as pl
from jax.experimental.pallas import tpu as pltpu
from jax.sharding import PartitionSpec as P

D = 6144
FF = 24576
TOKENS = 512
MESH = pl.DeviceIdType.MESH
F32, BF16 = jnp.float32, jnp.bfloat16

NZ, NY, NC, NN = 8, 4, 2, 8
ROWS = 8
BLOCK = NY * NC * ROWS
NX = 4
GROUPS = ((0, 1), (1, 2), (3, 2), (5, 2), (7, 1))
PLACES = ((1152, 128, 0), (0, 256, 0), (0, 256, 128), (768, 128, 0), (1152, 128, 64))
ROUNDS = ((0, 768), (768, 384), (1152, 384))
SUM_COLUMNS = 1536
FIRST_Y = 7
STEPS = (
    "x0h1a11001x1h230a211h30240x231a3h41203a460x3b0410470",
    "x4133261b114337142346243b2v0v1724463b3w0w16473b4u0u1",
)
FEAT, HID = 768, 384

tanh_scale = math.sqrt(2.0 / math.pi)
cubic_weight = 0.044715


def gelu_parts(pre):
    inner = tanh_scale * (pre + cubic_weight * pre * pre * pre)
    tangent = jnp.tanh(inner)
    value = 0.5 * pre * (1.0 + tangent)
    slope = 0.5 * (1.0 + tangent) + 0.5 * pre * (1.0 - tangent * tangent) * tanh_scale * (
        1.0 + 3.0 * cubic_weight * pre * pre
    )
    return (value, slope)


def split(values):
    high = values.astype(BF16)
    return high, (values - high.astype(F32)).astype(BF16)


def product(left, right):
    return jnp.dot(left, right, preferred_element_type=F32)


def dot3(pair, high, low):
    rows = pair[0].shape[0]
    both = product(jnp.concatenate(pair, axis=0), high)
    return (both[:rows] + both[rows:]) + product(pair[0], low)


def remote(source, target, send, recv, wide, narrow):
    return pltpu.make_async_remote_copy(
        src_ref=source,
        dst_ref=target,
        send_sem=send,
        recv_sem=recv,
        device_id=(wide, narrow),
        device_id_type=MESH,
    )


def drain(ref, sem):
    pltpu.make_async_copy(ref, ref, sem).wait()


def kernel(
    x_ref, g_ref, w_in_ref, b_ref, w_out_ref,
    grad_in_ref, raw_in_ref, raw_out_ref, bias_in_ref, bias_out_ref, factor_ref,
    xg, part, relay, near, ag, gi, gi_core, gi_z, gi_y, gi_y_first, gi_z_last, sums,
    w_in_f, w_out_f, w_in_h, w_in_l, w_out_h, w_out_l, w_back_h, w_back_l,
    x_across, g_along, p_along, a_across, bias, b_here,
    load_sem, y_send, y_recv, z_send, z_recv, c_send, c_recv,
    f_send, f_recv, n_send, n_recv, a_send, a_one_recv, a_far_recv,
    gc_send, gc_recv, gz_send, gz_recv, gy_send, gy_recv, gyf_send, gyf_recv, gzl_send, gzl_recv,
    s_send, s_recv,
):
    wide = lax.axis_index("wide")
    n = lax.axis_index("narrow")
    z = lax.div(wide, NY * NC)
    y = lax.rem(lax.div(wide, NC), NY)
    c = lax.rem(wide, NC)

    yl = lax.div(n, NX)
    x = lax.rem(n, NX)
    right, left, far = (lax.rem(x + j, NX) for j in (1, 3, 2))
    over = (1 - yl) * NX + x

    def at(zz, yy, cc):
        return (zz * NY + yy) * NC + cc

    load_in = pltpu.make_async_copy(w_in_ref, w_in_f, load_sem.at[0])
    load_out = pltpu.make_async_copy(w_out_ref, w_out_f, load_sem.at[1])
    load_x = pltpu.make_async_copy(x_ref, xg.at[0, z, c, y], load_sem.at[2])
    load_g = pltpu.make_async_copy(g_ref, xg.at[1, z, c, y], load_sem.at[3])
    load_b = pltpu.make_async_copy(b_ref, b_here, load_sem.at[4])
    for load in (load_x, load_g, load_in, load_out, load_b):
        load.start()

    plane = lax.rem(wide, NY * NC)
    barrier = pltpu.get_barrier_semaphore()
    for j in range(1, 8):
        for peer in (
            (wide, lax.rem(n + j, NN)),
            (z * NY * NC + lax.rem(plane + j, NY * NC), n),
            (lax.rem(z + j, NZ) * NY * NC + plane, n),
        ):
            pl.semaphore_signal(barrier, inc=1, device_id=peer, device_id_type=MESH)
    load_x.wait()
    load_g.wait()
    pl.semaphore_wait(barrier, 21)

    def first_row(row):
        part_of = xg.at[:, z, c, row]
        for k in (1, 2):
            to = at(lax.rem(z + (NZ - 1 if k == 2 else 1), NZ), y, c)
            remote(part_of, part_of, z_send, z_recv.at[k, 0], to, n).start()
        remote(part_of, part_of, c_send, c_recv.at[0], at(z, y, 1 - c), n).start()

    def next_row(j):
        row = lax.rem(y + NY - j, NY)
        drain(xg.at[:, z, c, row], y_recv.at[j - 1])
        if j != 2:
            half = xg.at[j // 2, z, c, row]
            remote(half, half, y_send, y_recv.at[1], at(z, lax.rem(y + j, NY), c), n).start()
        first_row(row)

    own = xg.at[:, z, c, y]
    for j in (1, 3):
        remote(own, own, y_send, y_recv.at[j - 1], at(z, lax.rem(y + j, NY), c), n).start()
    first_row(y)
    load_in.wait()
    w_in_h[...], w_in_l[...] = split(w_in_f[...])
    next_row(1)
    next_row(3)
    load_out.wait()
    w_out_h[...], w_out_l[...] = split(w_out_f[...].T)
    load_b.wait()
    next_row(2)

    def block_of(k):
        return lax.rem(z + NZ + (1 - 2 * (k % 2)) * ((k + 1) // 2), NZ)

    def arrive(group, array):
        first, count = GROUPS[group]
        for k in range(first, first + count):
            here = xg.at[array, block_of(k), c]
            if group > 1:
                drain(here, z_recv.at[k, array])
            elif array == 0:
                drain(xg.at[:, block_of(k), c], z_recv.at[k, 0])
            if k < 5 or k - 5 == array:
                onward = at(lax.rem(z + NZ - 1 + 2 * (k % 2), NZ), y, c)
                remote(here, here, z_send, z_recv.at[k + 2 if k < 5 else 7, array], onward, n).start()
        for k in range(first, first + count):
            here = xg.at[array, block_of(k), c]
            remote(here, here, c_send, c_recv.at[k], at(z, y, 1 - c), n).start()

    def tokens(array, group):
        first, count = GROUPS[group]
        return jnp.concatenate(
            [xg[array, block_of(k)].reshape(BLOCK, FEAT) for k in range(first, first + count)], axis=0
        )

    def hidden(which, group):
        first, count = GROUPS[group]
        return jnp.concatenate(
            [ag[:, k, which].reshape(BLOCK, HID) for k in range(first, first + count)], axis=0
        )

    def forward(group):
        first, count = GROUPS[group]
        for k in range(first, first + count):
            drain(xg.at[:, block_of(k), 1 - c], c_recv.at[k])
        pre = dot3(split(tokens(0, group)), w_in_h[...], w_in_l[...])
        grad_act = dot3(split(tokens(1, group)), w_out_h[...], w_out_l[...])
        for b in range(count):
            rows = slice(b * BLOCK, (b + 1) * BLOCK)
            part[:, first + b, 0] = pre[rows].reshape(NN, ROWS, HID)
            part[:, first + b, 1] = grad_act[rows].reshape(NN, ROWS, HID)
        some = pl.ds(first, count)
        to_right, to_left = yl * NX + right, yl * NX + left
        remote(part.at[far, some], relay.at[0, some], f_send, f_recv.at[group], wide, to_right).start()
        remote(part.at[NX + far, some], relay.at[1, some], f_send, f_recv.at[group], wide, to_left).start()
        for owner, slot in ((NX + right, 3 - 2 * yl), (left, 2 + 2 * yl), (over, 0)):
            remote(part.at[owner, some], near.at[slot, some], n_send, n_recv.at[group], wide, owner).start()

    def keep_tokens(group):
        column, third, start = PLACES[group]
        size = GROUPS[group][1] * BLOCK
        across, along = split(tokens(0, group).T), split(tokens(1, group))
        for i in range(3):
            place = slice(column + third * i + start, column + third * i + start + size)
            x_across[:, place] = across[(0, 1, 0)[i]]
            g_along[place, :] = along[(0, 0, 1)[i]]

    def pass_on(group):
        some = pl.ds(*GROUPS[group])
        drain(relay.at[:, some], f_recv.at[group])
        part[right, some] += relay[0, some]
        part[NX + left, some] += relay[1, some]
        for owner, slot in ((right, 1 + 2 * yl), (NX + left, 4 - 2 * yl)):
            remote(part.at[owner, some], near.at[slot, some], n_send, n_recv.at[group], wide, owner).start()

    def activate(group):
        some = pl.ds(*GROUPS[group])
        drain(near.at[:, some], n_recv.at[group])
        total = part[n, some]
        for j in range(5):
            total = total + near[j, some]
        act, slope = gelu_parts(total[:, 0] + b_here[...])
        ag[n, some, 0] = act
        ag[n, some, 1] = total[:, 1] * slope
        mine = ag.at[n, some]
        for peer in (right, NX + right, left, NX + left, over):
            remote(mine, mine, a_send, a_one_recv.at[group], wide, peer).start()

    def spread(group):
        some = pl.ds(*GROUPS[group])
        drain(ag.at[pl.ds(0, 5), some], a_one_recv.at[group])
        for owner, peer in ((left, yl * NX + right), (NX + right, yl * NX + left)):
            chunk = ag.at[owner, some]
            remote(chunk, chunk, a_send, a_far_recv.at[group], wide, peer).start()

    def backward(group):
        first, count = GROUPS[group]
        some = pl.ds(first, count)
        drain(ag.at[pl.ds(0, 2), some], a_far_recv.at[group])
        grad = dot3(split(hidden(1, group)), w_back_h[...], w_back_l[...])
        gi[some] = grad.reshape(count, NC, NY, ROWS, FEAT)
        remote(
            gi.at[some, 1 - c], gi_core.at[some], gc_send, gc_recv.at[group], at(z, y, 1 - c), n
        ).start()

    def keep_hidden(group):
        column, third, start = PLACES[group]
        size = GROUPS[group][1] * BLOCK
        grad_pre = hidden(1, group)
        bias[...] += jnp.sum(grad_pre.reshape(size // 8, 8, HID), axis=0)
        across, along = split(hidden(0, group).T), split(grad_pre)
        for i in range(3):
            place = slice(column + third * i + start, column + third * i + start + size)
            a_across[:, place] = across[(0, 1, 0)[i]]
            p_along[place, :] = along[(0, 0, 1)[i]]

    def hand_over(group):
        first, count = GROUPS[group]
        drain(gi_core.at[pl.ds(first, count)], gc_recv.at[group])
        for k in range(first, first + count):
            gi[k, c] += gi_core[k]
            if 0 < k < FIRST_Y:
                remote(
                    gi.at[k, c], gi_z.at[k - 1], gz_send, gz_recv, at(block_of(k), y, c), n
                ).start()
        if first >= FIRST_Y:
            for j in (2, 1, 3):
                to = lax.rem(y + j, NY)
                remote(
                    gi.at[pl.ds(first, count), c, to],
                    gi_y_first.at[j - 1, pl.ds(first - FIRST_Y, count)],
                    gyf_send, gyf_recv, at(z, to, c), n,
                ).start()

    def to_owner(group):
        first, count = GROUPS[group]
        drain(gi_y_first, gyf_recv)
        for k in range(first, first + count):
            i = k - FIRST_Y
            gi[k, c, y] += gi_y_first[0, i] + (gi_y_first[1, i] + gi_y_first[2, i])
            remote(
                gi.at[k, c, y], gi_z_last.at[i], gzl_send, gzl_recv, at(block_of(k), y, c), n
            ).start()

    def to_vreg(squares):
        rows, columns = squares.shape
        lanes = jnp.sum(squares.reshape(rows // 8, 8, columns), axis=0)
        out = lanes[:, :128]
        for j in range(1, columns // 128):
            out = out + lanes[:, 128 * j:128 * (j + 1)]
        return out

    def weight_round(turn, size, across, along, raw):
        place = slice(ROUNDS[turn][0], sum(ROUNDS[turn]))
        total = jnp.zeros((8, 128), F32)
        for start in range(0, raw.shape[0], size):
            rows = slice(start, start + size)
            tile = product(across[rows, place], along[place, :])
            if turn > 0:
                tile = tile + raw[rows, :]
            if turn == 2:
                total = total + to_vreg(tile * tile)
            raw[rows, :] = tile
        return total

    totals = []

    def weights(turn):
        def one(which):
            if which == 0:
                total = weight_round(turn, 256, x_across, p_along, raw_in_ref)
            else:
                total = weight_round(turn, 128, a_across, g_along, raw_out_ref)
            if turn == 2:
                totals.append(total)

        return one

    bias[...] = jnp.zeros_like(bias)
    stages = {
        "h": lambda group: arrive(group, 0), "a": lambda group: arrive(group, 1),
        "0": forward, "1": pass_on, "3": activate, "4": spread,
        "6": backward, "7": hand_over, "x": keep_tokens, "b": keep_hidden,
        "v": weights(0), "w": weights(1), "u": weights(2),
    }
    w_back_h[...], w_back_l[...] = split(w_in_f[...].T)
    forward(0)
    for order in STEPS:
        for stage, which in zip(order[::2], order[1::2]):
            stages[stage](int(which))
    total = totals[0] + totals[1]

    def share(phase, place, value, peers):
        sums[phase, place] = value
        for peer in peers:
            slot = sums.at[phase, place]
            remote(slot, slot, s_send, s_recv.at[phase], *peer).start()

    def collect(phase):
        drain(sums.at[phase, pl.ds(0, 7)], s_recv.at[phase])
        return jnp.sum(sums[phase], axis=0)

    share(0, n, total, [(wide, lax.rem(n + j, NN)) for j in range(1, 8)])

    hand_over(4)
    total = collect(0)
    share(1, plane, total, [
        (z * NY * NC + lax.rem(plane + j, NY * NC), n) for j in range(1, 8)
    ])
    to_owner(4)
    drain(gi_z, gz_recv)
    own_sum = gi[0, c]
    for j in range(FIRST_Y - 1):
        own_sum = own_sum + gi_z[j]
    gi[0, c] = own_sum
    for j in (2, 1, 3):
        to = lax.rem(y + j, NY)
        remote(gi.at[0, c, to], gi_y.at[j - 1], gy_send, gy_recv, at(z, to, c), n).start()
    bias_in_ref[...] = jnp.sum(bias[...], axis=0, keepdims=True)
    bias_out_ref[...] = jnp.sum(xg[1].reshape(TOKENS, FEAT), axis=0, keepdims=True)
    total = collect(1)
    share(2, z, total, [
        (lax.rem(z + j, NZ) * NY * NC + plane, n) for j in range(1, 8)
    ])
    drain(gi_y, gy_recv)
    drain(gi_z_last, gzl_recv)
    grad_in_ref[...] = ((gi[0, c, y] + gi_y[0]) + (gi_y[1] + gi_y[2])) + gi_z_last[0]
    drain(xg.at[:, z, c, pl.ds(0, 3)], y_send)
    drain(xg.at[:, pl.ds(0, 7), 0], z_send)
    drain(xg.at[:, :, 0], c_send)
    drain(relay, f_send)
    drain(near, n_send)
    drain(ag.at[pl.ds(0, 7)], a_send)
    drain(gi_core, gc_send)
    drain(gi_z, gz_send)
    drain(gi_y, gy_send)
    drain(gi_y_first, gyf_send)
    drain(gi_z_last, gzl_send)
    total = jnp.sum(collect(2), keepdims=True)
    factor = jnp.minimum(1.0, math.sqrt(1.0 * D * FF * TOKENS) / (jnp.sqrt(total) + 1e-06))
    factor_ref[...] = jnp.broadcast_to(factor, factor_ref.shape)
    drain(sums.at[:, pl.ds(0, 7)], s_send)


PIECES = 3


def scale_kernel(
    grad_in_ref, raw_in_ref, raw_out_ref, bias_in_ref, bias_out_ref, factor_ref,
    grad_in_out, gw_in, gw_out, gb_in, gb_out, buf_in, buf_out, bias_in, bias_out, sems, small_sems,
):
    factor = factor_ref[0:1, 0:1]
    bias_in[...] = (bias_in_ref[...] * factor)[0]
    bias_out[...] = (bias_out_ref[...] * factor)[0]
    stores = []
    for i, (source, out) in enumerate(
        ((grad_in_ref, grad_in_out), (bias_in, gb_in), (bias_out, gb_out))
    ):
        store = pltpu.make_async_copy(source, out, small_sems.at[i])
        store.start()
        stores.append(store)
    for which, (raw, buf, out) in enumerate(
        ((raw_in_ref, buf_in, gw_in), (raw_out_ref, buf_out, gw_out))
    ):
        size = raw.shape[0] // PIECES
        for i in range(PIECES):
            rows = pl.ds(i * size, size)
            buf[rows, :] = raw[rows, :] * factor
            store = pltpu.make_async_copy(buf.at[rows], out.at[rows], sems.at[which, i])
            store.start()
            stores.append(store)
    for store in stores:
        store.wait()


def local(x_tokens, grad_out, w_in, b_in, w_out):
    vmem = pl.BlockSpec(memory_space=pltpu.VMEM)
    anywhere = pl.BlockSpec(memory_space=pl.ANY)
    dma = pltpu.SemaphoreType.DMA
    grad_in, raw_in, raw_out, bias_in, bias_out, factor = pl.pallas_call(
        kernel,
        out_shape=(
            jax.ShapeDtypeStruct((ROWS, FEAT), F32),
            jax.ShapeDtypeStruct((FEAT, HID), F32),
            jax.ShapeDtypeStruct((HID, FEAT), F32),
            jax.ShapeDtypeStruct((1, HID), F32),
            jax.ShapeDtypeStruct((1, FEAT), F32),
            jax.ShapeDtypeStruct((8, 128), F32),
        ),
        in_specs=[pl.BlockSpec(memory_space=pltpu.HBM)] * 5,
        out_specs=(vmem, vmem, vmem, vmem, vmem, vmem),
        scratch_shapes=[
            pltpu.VMEM((2, NZ, NC, NY, ROWS, FEAT), F32),
            pltpu.VMEM((NN, NZ, 2, ROWS, HID), F32),
            pltpu.VMEM((2, NZ, 2, ROWS, HID), F32),
            pltpu.VMEM((5, NZ, 2, ROWS, HID), F32),
            pltpu.VMEM((NN, NZ, 2, ROWS, HID), F32),
            pltpu.VMEM((NZ, NC, NY, ROWS, FEAT), F32),
            pltpu.VMEM((NZ, NY, ROWS, FEAT), F32),
            pltpu.VMEM((FIRST_Y - 1, NY, ROWS, FEAT), F32),
            pltpu.VMEM((NY - 1, ROWS, FEAT), F32),
            pltpu.VMEM((NY - 1, NZ - FIRST_Y, ROWS, FEAT), F32),
            pltpu.VMEM((NZ - FIRST_Y, ROWS, FEAT), F32),
            pltpu.VMEM((3, 8, 8, 128), F32),
            pltpu.VMEM((FEAT, HID), F32),
            pltpu.VMEM((HID, FEAT), F32),
            pltpu.VMEM((FEAT, HID), BF16),
            pltpu.VMEM((FEAT, HID), BF16),
            pltpu.VMEM((FEAT, HID), BF16),
            pltpu.VMEM((FEAT, HID), BF16),
            pltpu.VMEM((HID, FEAT), BF16),
            pltpu.VMEM((HID, FEAT), BF16),
            pltpu.VMEM((FEAT, SUM_COLUMNS), BF16),
            pltpu.VMEM((SUM_COLUMNS, FEAT), BF16),
            pltpu.VMEM((SUM_COLUMNS, HID), BF16),
            pltpu.VMEM((HID, SUM_COLUMNS), BF16),
            pltpu.VMEM((ROWS, HID), F32),
            pltpu.VMEM((HID,), F32),
            dma((5,)),
            dma, dma((NY - 1,)),
            dma, dma((NZ, 2)),
            dma, dma((NZ,)),
            dma, dma((5,)),
            dma, dma((5,)),
            dma, dma((5,)), dma((5,)),
            dma, dma((5,)),
            dma, dma,
            dma, dma,
            dma, dma,
            dma, dma,
            dma, dma((3,)),
        ],
        compiler_params=pltpu.CompilerParams(
            collective_id=0, has_side_effects=True, vmem_limit_bytes=51 * 1024 * 1024
        ),
    )(*(pltpu.with_memory_space_constraint(a, pltpu.HBM) for a in (x_tokens, grad_out, w_in, b_in, w_out)))
    return pl.pallas_call(
        scale_kernel,
        out_shape=(
            jax.ShapeDtypeStruct((ROWS, FEAT), F32),
            jax.ShapeDtypeStruct((FEAT, HID), F32),
            jax.ShapeDtypeStruct((HID, FEAT), F32),
            jax.ShapeDtypeStruct((HID,), F32),
            jax.ShapeDtypeStruct((FEAT,), F32),
        ),
        in_specs=[vmem, vmem, vmem, vmem, vmem, vmem],
        out_specs=(anywhere,) * 5,
        scratch_shapes=[
            pltpu.VMEM((FEAT, HID), F32),
            pltpu.VMEM((HID, FEAT), F32),
            pltpu.VMEM((HID,), F32),
            pltpu.VMEM((FEAT,), F32),
            dma((2, PIECES)),
            dma((3,)),
        ],
        compiler_params=pltpu.CompilerParams(vmem_limit_bytes=16 * 1024 * 1024),
    )(grad_in, raw_in, raw_out, bias_in, bias_out, factor)


def solution(mesh):
    placed = (
        P("wide", "narrow"),
        P("wide", "narrow"),
        P("narrow", "wide"),
        P("wide"),
        P("wide", "narrow"),
    )
    return jax.shard_map(
        local,
        mesh=mesh,
        in_specs=placed,
        out_specs=(
            P("wide", "narrow"),
            P("narrow", "wide"),
            P("wide", "narrow"),
            P("wide"),
            P("narrow"),
        ),
        check_vma=False,
    )
```

```python
import math

import jax
import jax.numpy as jnp
from jax import lax
from jax.experimental import pallas as pl
from jax.experimental.pallas import tpu as pltpu
from jax.sharding import PartitionSpec as P

D = 6144
FF = 24576
TOKENS = 512
MESH = pl.DeviceIdType.MESH
F32, BF16 = jnp.float32, jnp.bfloat16

NZ, NY, NC, NN = 8, 4, 2, 8
ROWS = 8
BLOCK = NY * NC * ROWS
NX = 4
GROUPS = ((0, 1), (1, 2), (3, 2), (5, 2), (7, 1))
PLACES = ((1152, 128, 0), (0, 256, 0), (0, 256, 128), (768, 128, 0), (1152, 128, 64))
ROUNDS = ((0, 768), (768, 384), (1152, 384))
SUM_COLUMNS = 1536
STEPS = (
    "x0h1a11001x1h230a211h30240x231a3h41203a460x3b0410470",
    "x4133261b114337142346243b2v0v1724463b3w0w16473b4u0u1",
)
FEAT, HID = 768, 384

tanh_scale = math.sqrt(2.0 / math.pi)
cubic_weight = 0.044715


def gelu_parts(pre):
    inner = tanh_scale * (pre + cubic_weight * pre * pre * pre)
    tangent = jnp.tanh(inner)
    value = 0.5 * pre * (1.0 + tangent)
    slope = 0.5 * (1.0 + tangent) + 0.5 * pre * (1.0 - tangent * tangent) * tanh_scale * (
        1.0 + 3.0 * cubic_weight * pre * pre
    )
    return (value, slope)


def split(values):
    high = values.astype(BF16)
    return high, (values - high.astype(F32)).astype(BF16)


def product(left, right):
    return jnp.dot(left, right, preferred_element_type=F32)


def dot3(pair, high, low):
    rows = pair[0].shape[0]
    both = product(jnp.concatenate(pair, axis=0), high)
    return (both[:rows] + both[rows:]) + product(pair[0], low)


def remote(source, target, send, recv, wide, narrow):
    return pltpu.make_async_remote_copy(
        src_ref=source,
        dst_ref=target,
        send_sem=send,
        recv_sem=recv,
        device_id=(wide, narrow),
        device_id_type=MESH,
    )


def drain(ref, sem):
    pltpu.make_async_copy(ref, ref, sem).wait()


def kernel(
    x_ref, g_ref, w_in_ref, b_ref, w_out_ref,
    grad_in_ref, raw_in_ref, raw_out_ref, bias_in_ref, bias_out_ref, factor_ref,
    xg, part, relay, near, ag, gi, gi_core, gi_z, gi_y, sums,
    w_in_f, w_out_f, w_in_h, w_in_l, w_out_h, w_out_l, w_back_h, w_back_l,
    x_across, g_along, p_along, a_across, bias, b_here,
    load_sem, y_send, y_recv, z_send, z_recv, c_send, c_recv,
    f_send, f_recv, n_send, n_recv, a_send, a_one_recv, a_far_recv,
    gc_send, gc_recv, gz_send, gz_recv, gy_send, gy_recv,
    s_send, s_recv,
):
    wide = lax.axis_index("wide")
    n = lax.axis_index("narrow")
    z = lax.div(wide, NY * NC)
    y = lax.rem(lax.div(wide, NC), NY)
    c = lax.rem(wide, NC)

    yl = lax.div(n, NX)
    x = lax.rem(n, NX)
    right, left, far = (lax.rem(x + j, NX) for j in (1, 3, 2))
    over = (1 - yl) * NX + x

    def at(zz, yy, cc):
        return (zz * NY + yy) * NC + cc

    load_in = pltpu.make_async_copy(w_in_ref, w_in_f, load_sem.at[0])
    load_out = pltpu.make_async_copy(w_out_ref, w_out_f, load_sem.at[1])
    load_x = pltpu.make_async_copy(x_ref, xg.at[0, z, c, y], load_sem.at[2])
    load_g = pltpu.make_async_copy(g_ref, xg.at[1, z, c, y], load_sem.at[3])
    load_b = pltpu.make_async_copy(b_ref, b_here, load_sem.at[4])
    for load in (load_x, load_g, load_in, load_out, load_b):
        load.start()

    plane = lax.rem(wide, NY * NC)
    barrier = pltpu.get_barrier_semaphore()
    for j in range(1, 8):
        for peer in (
            (wide, lax.rem(n + j, NN)),
            (z * NY * NC + lax.rem(plane + j, NY * NC), n),
            (lax.rem(z + j, NZ) * NY * NC + plane, n),
        ):
            pl.semaphore_signal(barrier, inc=1, device_id=peer, device_id_type=MESH)
    load_x.wait()
    load_g.wait()
    pl.semaphore_wait(barrier, 21)

    def first_row(row):
        part_of = xg.at[:, z, c, row]
        for k in (1, 2):
            to = at(lax.rem(z + (NZ - 1 if k == 2 else 1), NZ), y, c)
            remote(part_of, part_of, z_send, z_recv.at[k, 0], to, n).start()
        remote(part_of, part_of, c_send, c_recv.at[0], at(z, y, 1 - c), n).start()

    def next_row(j):
        row = lax.rem(y + NY - j, NY)
        drain(xg.at[:, z, c, row], y_recv.at[j - 1])
        first_row(row)

    own = xg.at[:, z, c, y]
    for j in (1, 3, 2):
        remote(own, own, y_send, y_recv.at[j - 1], at(z, lax.rem(y + j, NY), c), n).start()
    first_row(y)
    load_in.wait()
    w_in_h[...], w_in_l[...] = split(w_in_f[...])
    next_row(1)
    next_row(3)
    load_out.wait()
    w_out_h[...], w_out_l[...] = split(w_out_f[...].T)
    load_b.wait()
    next_row(2)

    def block_of(k):
        return lax.rem(z + NZ + (1 - 2 * (k % 2)) * ((k + 1) // 2), NZ)

    def arrive(group, array):
        first, count = GROUPS[group]
        for k in range(first, first + count):
            here = xg.at[array, block_of(k), c]
            if group > 1:
                drain(here, z_recv.at[k, array])
            elif array == 0:
                drain(xg.at[:, block_of(k), c], z_recv.at[k, 0])
            if k < 5 or k - 5 == array:
                onward = at(lax.rem(z + NZ - 1 + 2 * (k % 2), NZ), y, c)
                remote(here, here, z_send, z_recv.at[k + 2 if k < 5 else 7, array], onward, n).start()
        for k in range(first, first + count):
            here = xg.at[array, block_of(k), c]
            remote(here, here, c_send, c_recv.at[k], at(z, y, 1 - c), n).start()

    def tokens(array, group):
        first, count = GROUPS[group]
        return jnp.concatenate(
            [xg[array, block_of(k)].reshape(BLOCK, FEAT) for k in range(first, first + count)], axis=0
        )

    def hidden(which, group):
        first, count = GROUPS[group]
        return jnp.concatenate(
            [ag[:, k, which].reshape(BLOCK, HID) for k in range(first, first + count)], axis=0
        )

    def forward(group):
        first, count = GROUPS[group]
        for k in range(first, first + count):
            drain(xg.at[:, block_of(k), 1 - c], c_recv.at[k])
        pre = dot3(split(tokens(0, group)), w_in_h[...], w_in_l[...])
        grad_act = dot3(split(tokens(1, group)), w_out_h[...], w_out_l[...])
        for b in range(count):
            rows = slice(b * BLOCK, (b + 1) * BLOCK)
            part[:, first + b, 0] = pre[rows].reshape(NN, ROWS, HID)
            part[:, first + b, 1] = grad_act[rows].reshape(NN, ROWS, HID)
        some = pl.ds(first, count)
        to_right, to_left = yl * NX + right, yl * NX + left
        remote(part.at[far, some], relay.at[0, some], f_send, f_recv.at[group], wide, to_right).start()
        remote(part.at[NX + far, some], relay.at[1, some], f_send, f_recv.at[group], wide, to_left).start()
        for owner, slot in ((NX + right, 3 - 2 * yl), (left, 2 + 2 * yl), (over, 0)):
            remote(part.at[owner, some], near.at[slot, some], n_send, n_recv.at[group], wide, owner).start()

    def keep_tokens(group):
        column, third, start = PLACES[group]
        size = GROUPS[group][1] * BLOCK
        across, along = split(tokens(0, group).T), split(tokens(1, group))
        for i in range(3):
            place = slice(column + third * i + start, column + third * i + start + size)
            x_across[:, place] = across[(0, 1, 0)[i]]
            g_along[place, :] = along[(0, 0, 1)[i]]

    def pass_on(group):
        some = pl.ds(*GROUPS[group])
        drain(relay.at[:, some], f_recv.at[group])
        part[right, some] += relay[0, some]
        part[NX + left, some] += relay[1, some]
        for owner, slot in ((right, 1 + 2 * yl), (NX + left, 4 - 2 * yl)):
            remote(part.at[owner, some], near.at[slot, some], n_send, n_recv.at[group], wide, owner).start()

    def activate(group):
        some = pl.ds(*GROUPS[group])
        drain(near.at[:, some], n_recv.at[group])
        total = part[n, some]
        for j in range(5):
            total = total + near[j, some]
        act, slope = gelu_parts(total[:, 0] + b_here[...])
        ag[n, some, 0] = act
        ag[n, some, 1] = total[:, 1] * slope
        mine = ag.at[n, some]
        for peer in (right, NX + right, left, NX + left, over):
            remote(mine, mine, a_send, a_one_recv.at[group], wide, peer).start()

    def spread(group):
        some = pl.ds(*GROUPS[group])
        drain(ag.at[pl.ds(0, 5), some], a_one_recv.at[group])
        for owner, peer in ((left, yl * NX + right), (NX + right, yl * NX + left)):
            chunk = ag.at[owner, some]
            remote(chunk, chunk, a_send, a_far_recv.at[group], wide, peer).start()

    def backward(group):
        first, count = GROUPS[group]
        some = pl.ds(first, count)
        drain(ag.at[pl.ds(0, 2), some], a_far_recv.at[group])
        grad = dot3(split(hidden(1, group)), w_back_h[...], w_back_l[...])
        gi[some] = grad.reshape(count, NC, NY, ROWS, FEAT)
        remote(
            gi.at[some, 1 - c], gi_core.at[some], gc_send, gc_recv.at[group], at(z, y, 1 - c), n
        ).start()

    def keep_hidden(group):
        column, third, start = PLACES[group]
        size = GROUPS[group][1] * BLOCK
        grad_pre = hidden(1, group)
        bias[...] += jnp.sum(grad_pre.reshape(size // 8, 8, HID), axis=0)
        across, along = split(hidden(0, group).T), split(grad_pre)
        for i in range(3):
            place = slice(column + third * i + start, column + third * i + start + size)
            a_across[:, place] = across[(0, 1, 0)[i]]
            p_along[place, :] = along[(0, 0, 1)[i]]

    def hand_over(group):
        first, count = GROUPS[group]
        drain(gi_core.at[pl.ds(first, count)], gc_recv.at[group])
        for k in range(first, first + count):
            gi[k, c] += gi_core[k]
            if k > 0:
                remote(
                    gi.at[k, c], gi_z.at[k - 1], gz_send, gz_recv, at(block_of(k), y, c), n
                ).start()

    def to_vreg(squares):
        rows, columns = squares.shape
        lanes = jnp.sum(squares.reshape(rows // 8, 8, columns), axis=0)
        out = lanes[:, :128]
        for j in range(1, columns // 128):
            out = out + lanes[:, 128 * j:128 * (j + 1)]
        return out

    def weight_round(turn, size, across, along, raw):
        place = slice(ROUNDS[turn][0], sum(ROUNDS[turn]))
        total = jnp.zeros((8, 128), F32)
        for start in range(0, raw.shape[0], size):
            rows = slice(start, start + size)
            tile = product(across[rows, place], along[place, :])
            if turn > 0:
                tile = tile + raw[rows, :]
            if turn == 2:
                total = total + to_vreg(tile * tile)
            raw[rows, :] = tile
        return total

    totals = []

    def weights(turn):
        def one(which):
            if which == 0:
                total = weight_round(turn, 256, x_across, p_along, raw_in_ref)
            else:
                total = weight_round(turn, 128, a_across, g_along, raw_out_ref)
            if turn == 2:
                totals.append(total)

        return one

    bias[...] = jnp.zeros_like(bias)
    stages = {
        "h": lambda group: arrive(group, 0), "a": lambda group: arrive(group, 1),
        "0": forward, "1": pass_on, "3": activate, "4": spread,
        "6": backward, "7": hand_over, "x": keep_tokens, "b": keep_hidden,
        "v": weights(0), "w": weights(1), "u": weights(2),
    }
    w_back_h[...], w_back_l[...] = split(w_in_f[...].T)
    forward(0)
    for order in STEPS:
        for stage, which in zip(order[::2], order[1::2]):
            stages[stage](int(which))
    total = totals[0] + totals[1]

    def share(phase, place, value, peers):
        sums[phase, place] = value
        for peer in peers:
            slot = sums.at[phase, place]
            remote(slot, slot, s_send, s_recv.at[phase], *peer).start()

    def collect(phase):
        drain(sums.at[phase, pl.ds(0, 7)], s_recv.at[phase])
        return jnp.sum(sums[phase], axis=0)

    share(0, n, total, [(wide, lax.rem(n + j, NN)) for j in range(1, 8)])

    hand_over(4)
    total = collect(0)
    share(1, plane, total, [
        (z * NY * NC + lax.rem(plane + j, NY * NC), n) for j in range(1, 8)
    ])
    drain(gi_z, gz_recv)
    own_sum = gi[0, c]
    for j in range(NZ - 1):
        own_sum = own_sum + gi_z[j]
    gi[0, c] = own_sum
    for j in (2, 1, 3):
        to = lax.rem(y + j, NY)
        remote(gi.at[0, c, to], gi_y.at[j - 1], gy_send, gy_recv, at(z, to, c), n).start()
    bias_in_ref[...] = jnp.sum(bias[...], axis=0, keepdims=True)
    bias_out_ref[...] = jnp.sum(xg[1].reshape(TOKENS, FEAT), axis=0, keepdims=True)
    total = collect(1)
    share(2, z, total, [
        (lax.rem(z + j, NZ) * NY * NC + plane, n) for j in range(1, 8)
    ])
    drain(gi_y, gy_recv)
    grad_in_ref[...] = (gi[0, c, y] + gi_y[0]) + (gi_y[1] + gi_y[2])
    drain(xg.at[:, z, c, pl.ds(0, 3)], y_send)
    drain(xg.at[:, pl.ds(0, 7), 0], z_send)
    drain(xg.at[:, :, 0], c_send)
    drain(relay, f_send)
    drain(near, n_send)
    drain(ag.at[pl.ds(0, 7)], a_send)
    drain(gi_core, gc_send)
    drain(gi_z, gz_send)
    drain(gi_y, gy_send)
    total = jnp.sum(collect(2), keepdims=True)
    factor = jnp.minimum(1.0, math.sqrt(1.0 * D * FF * TOKENS) / (jnp.sqrt(total) + 1e-06))
    factor_ref[...] = jnp.broadcast_to(factor, factor_ref.shape)
    drain(sums.at[:, pl.ds(0, 7)], s_send)


PIECES = 3


def scale_kernel(
    grad_in_ref, raw_in_ref, raw_out_ref, bias_in_ref, bias_out_ref, factor_ref,
    grad_in_out, gw_in, gw_out, gb_in, gb_out, buf_in, buf_out, bias_in, bias_out, sems, small_sems,
):
    factor = factor_ref[0:1, 0:1]
    bias_in[...] = (bias_in_ref[...] * factor)[0]
    bias_out[...] = (bias_out_ref[...] * factor)[0]
    stores = []
    for i, (source, out) in enumerate(
        ((grad_in_ref, grad_in_out), (bias_in, gb_in), (bias_out, gb_out))
    ):
        store = pltpu.make_async_copy(source, out, small_sems.at[i])
        store.start()
        stores.append(store)
    for which, (raw, buf, out) in enumerate(
        ((raw_in_ref, buf_in, gw_in), (raw_out_ref, buf_out, gw_out))
    ):
        size = raw.shape[0] // PIECES
        for i in range(PIECES):
            rows = pl.ds(i * size, size)
            buf[rows, :] = raw[rows, :] * factor
            store = pltpu.make_async_copy(buf.at[rows], out.at[rows], sems.at[which, i])
            store.start()
            stores.append(store)
    for store in stores:
        store.wait()


def local(x_tokens, grad_out, w_in, b_in, w_out):
    vmem = pl.BlockSpec(memory_space=pltpu.VMEM)
    anywhere = pl.BlockSpec(memory_space=pl.ANY)
    dma = pltpu.SemaphoreType.DMA
    grad_in, raw_in, raw_out, bias_in, bias_out, factor = pl.pallas_call(
        kernel,
        out_shape=(
            jax.ShapeDtypeStruct((ROWS, FEAT), F32),
            jax.ShapeDtypeStruct((FEAT, HID), F32),
            jax.ShapeDtypeStruct((HID, FEAT), F32),
            jax.ShapeDtypeStruct((1, HID), F32),
            jax.ShapeDtypeStruct((1, FEAT), F32),
            jax.ShapeDtypeStruct((8, 128), F32),
        ),
        in_specs=[pl.BlockSpec(memory_space=pltpu.HBM)] * 5,
        out_specs=(vmem, vmem, vmem, vmem, vmem, vmem),
        scratch_shapes=[
            pltpu.VMEM((2, NZ, NC, NY, ROWS, FEAT), F32),
            pltpu.VMEM((NN, NZ, 2, ROWS, HID), F32),
            pltpu.VMEM((2, NZ, 2, ROWS, HID), F32),
            pltpu.VMEM((5, NZ, 2, ROWS, HID), F32),
            pltpu.VMEM((NN, NZ, 2, ROWS, HID), F32),
            pltpu.VMEM((NZ, NC, NY, ROWS, FEAT), F32),
            pltpu.VMEM((NZ, NY, ROWS, FEAT), F32),
            pltpu.VMEM((NZ - 1, NY, ROWS, FEAT), F32),
            pltpu.VMEM((NY - 1, ROWS, FEAT), F32),
            pltpu.VMEM((3, 8, 8, 128), F32),
            pltpu.VMEM((FEAT, HID), F32),
            pltpu.VMEM((HID, FEAT), F32),
            pltpu.VMEM((FEAT, HID), BF16),
            pltpu.VMEM((FEAT, HID), BF16),
            pltpu.VMEM((FEAT, HID), BF16),
            pltpu.VMEM((FEAT, HID), BF16),
            pltpu.VMEM((HID, FEAT), BF16),
            pltpu.VMEM((HID, FEAT), BF16),
            pltpu.VMEM((FEAT, SUM_COLUMNS), BF16),
            pltpu.VMEM((SUM_COLUMNS, FEAT), BF16),
            pltpu.VMEM((SUM_COLUMNS, HID), BF16),
            pltpu.VMEM((HID, SUM_COLUMNS), BF16),
            pltpu.VMEM((ROWS, HID), F32),
            pltpu.VMEM((HID,), F32),
            dma((5,)),
            dma, dma((NY - 1,)),
            dma, dma((NZ, 2)),
            dma, dma((NZ,)),
            dma, dma((5,)),
            dma, dma((5,)),
            dma, dma((5,)), dma((5,)),
            dma, dma((5,)),
            dma, dma,
            dma, dma,
            dma, dma((3,)),
        ],
        compiler_params=pltpu.CompilerParams(
            collective_id=0, has_side_effects=True, vmem_limit_bytes=51 * 1024 * 1024
        ),
    )(*(pltpu.with_memory_space_constraint(a, pltpu.HBM) for a in (x_tokens, grad_out, w_in, b_in, w_out)))
    return pl.pallas_call(
        scale_kernel,
        out_shape=(
            jax.ShapeDtypeStruct((ROWS, FEAT), F32),
            jax.ShapeDtypeStruct((FEAT, HID), F32),
            jax.ShapeDtypeStruct((HID, FEAT), F32),
            jax.ShapeDtypeStruct((HID,), F32),
            jax.ShapeDtypeStruct((FEAT,), F32),
        ),
        in_specs=[vmem, vmem, vmem, vmem, vmem, vmem],
        out_specs=(anywhere,) * 5,
        scratch_shapes=[
            pltpu.VMEM((FEAT, HID), F32),
            pltpu.VMEM((HID, FEAT), F32),
            pltpu.VMEM((HID,), F32),
            pltpu.VMEM((FEAT,), F32),
            dma((2, PIECES)),
            dma((3,)),
        ],
        compiler_params=pltpu.CompilerParams(vmem_limit_bytes=16 * 1024 * 1024),
    )(grad_in, raw_in, raw_out, bias_in, bias_out, factor)


def solution(mesh):
    placed = (
        P("wide", "narrow"),
        P("wide", "narrow"),
        P("narrow", "wide"),
        P("wide"),
        P("wide", "narrow"),
    )
    return jax.shard_map(
        local,
        mesh=mesh,
        in_specs=placed,
        out_specs=(
            P("wide", "narrow"),
            P("narrow", "wide"),
            P("wide", "narrow"),
            P("wide"),
            P("narrow"),
        ),
        check_vma=False,
    )
```
